32 devices in a mesh: rows: 4 (over z), cols: 8 (over y, x, core).
Axes of the slice: x: 2, y: 2, z: 4, core: 2. Of those that a mesh axis runs over, the one named last changes fastest.
Arguments:
- pixels: bfloat16 [3, 512, 2048], P(None, 'rows', 'cols'), may hold values from -6 to 6
- patch_weight: bfloat16 [48, 256], replicated, may hold values from -0.875 to 0.875
- patch_bias: float32 [256], replicated, may hold values from -4 to 4
- conv_kernel: float32 [49, 256], replicated, may hold values from -0.875 to 0.875
- norm_gain: float32 [256], replicated, may hold values from 0.1 to 1.9
- kv_weight: bfloat16 [256, 2048], replicated, may hold values from -0.375 to 0.375
- latents: bfloat16 [256, 1024], replicated, may hold values from -80 to 80, as said below
- d_attended: bfloat16 [256, 1024], replicated, may hold values from -6 to 6
Outputs:
- attended: float32 [256, 1024], replicated
- grad_latents: float32 [256, 1024], replicated
- grad_kv_weight: float32 [256, 2048], replicated
- grad_norm_gain: float32 [256], replicated
- grad_conv_kernel: float32 [49, 256], replicated
- grad_patch_weight: float32 [48, 256], replicated
- grad_patch_bias: float32 [256], replicated
The draws below stay inside these ranges and needn't reach their ends.
Inputs may be any that keep to these rules, and one draw needn't show every extreme that they name: `latents`: each latent row has its own scale.
All inputs are finite; a program needn't handle non-finite values.
Results may differ from the reference program's by a relative error of at most 0.035.
The reference program's roundings to bfloat16 on the way count: a program that leaves them out, or rounds other values in their place, can miss the bound.
Values may be sent and summed in bfloat16 or wider, within the bound.
A program may use at most 576 MiB of HBM per device.

```python
import math
import jax
import jax.numpy as jnp
from jax import lax

PATCH = 4
KSIZE = 7
IN_CHANNELS = 3
CHANNELS = 256
HEADS = 8
DIM = 1024
LATENTS = 256
IMG_H = 512
IMG_W = 2048


def draw_latents(key, part):
    key_rows = jax.random.fold_in(key, 11)
    key_vals = jax.random.fold_in(key, 12)
    row_scale = jnp.exp(jax.random.uniform(key_rows, (LATENTS, 1), jnp.float32, math.log(0.3), math.log(3.0)))
    entries = jax.random.truncated_normal(key_vals, -4.0, 4.0, (LATENTS, DIM), jnp.float32)
    return (entries * row_scale).astype(jnp.bfloat16)


def block_levels(stream_key, extent, shards, smallest, top_value):
    def one(position, parts):
        draws = jax.random.uniform(jax.random.fold_in(jax.random.fold_in(stream_key, 6), position), (parts,), jnp.float32, smallest / len(shards), top_value / len(shards))
        return jnp.repeat(jnp.exp(draws), extent[position] // parts).reshape((-1,) + (1,) * (len(extent) - position - 1))

    factor_of = one(*shards[0])
    for cut in shards[1:]:
        factor_of = factor_of * one(*cut)
    return factor_of


def gaussian(own_key, dims, spread, reach, shards=(), held_as=jnp.bfloat16):
    values = jax.random.normal(own_key, dims, jnp.float32) * spread
    if len(shards) > 0:
        values = block_levels(own_key, dims, shards, -0.22, 0.18) * values
    return jnp.clip(values, min=-reach, max=reach).astype(held_as)


def setup_inputs(seed: int = 0) -> dict:
    keys = jax.random.split(jax.random.key(seed), 9)
    pixels = gaussian(keys[0], (IN_CHANNELS, IMG_H, IMG_W), 1.0, 6.0, ((1, 4), (2, 8)))
    patch_weight = gaussian(keys[1], (IN_CHANNELS * PATCH * PATCH, CHANNELS), (IN_CHANNELS * PATCH * PATCH) ** -0.5, 0.875)
    patch_bias = gaussian(keys[2], (CHANNELS,), 1.0, 4.0, (), jnp.float32)
    conv_kernel = gaussian(keys[3], (KSIZE * KSIZE, CHANNELS), (KSIZE * KSIZE) ** -0.5, 0.875, (), jnp.float32)
    norm_gain = jnp.clip(1.0 + 0.18 * jax.random.normal(keys[4], (CHANNELS,), jnp.float32), 0.1, 1.9)
    kv_weight = gaussian(keys[5], (CHANNELS, 2 * DIM), CHANNELS ** -0.5, 0.375)
    latents = draw_latents(jax.random.fold_in(keys[8], 71), 0)
    d_attended = gaussian(keys[7], (LATENTS, DIM), 1.0, 6.0)
    return {"pixels": pixels, "patch_weight": patch_weight, "patch_bias": patch_bias, "conv_kernel": conv_kernel, "norm_gain": norm_gain, "kv_weight": kv_weight, "latents": latents, "d_attended": d_attended}


norm_eps = 1e-05

def patch_rows(pixels):
    in_channels, height, image_width = pixels.shape
    blocks = pixels.reshape(in_channels, height // PATCH, PATCH, image_width // PATCH, PATCH)
    blocks = blocks.transpose(1, 3, 0, 2, 4)
    return blocks.reshape(height // PATCH * (image_width // PATCH), in_channels * PATCH * PATCH)

def depthwise(padded, kernel, tile_rows, tile_cols):
    result = jnp.zeros((tile_rows, tile_cols, kernel.shape[1]), jnp.float32)
    for offset_row in range(KSIZE):
        for offset_col in range(KSIZE):
            window = padded[offset_row:offset_row + tile_rows, offset_col:offset_col + tile_cols].astype(jnp.float32)
            result = result + window * kernel[offset_row * KSIZE + offset_col]
    return result

def transposed(padded, kernel, tile_rows, tile_cols):
    result = jnp.zeros((tile_rows, tile_cols, kernel.shape[1]), jnp.float32)
    last = KSIZE - 1
    for offset_row in range(KSIZE):
        for offset_col in range(KSIZE):
            start_row = last - offset_row
            start_col = last - offset_col
            window = padded[start_row:start_row + tile_rows, start_col:start_col + tile_cols].astype(jnp.float32)
            result = result + window * kernel[offset_row * KSIZE + offset_col]
    return result

def kernel_grad(padded, upstream, tile_rows, tile_cols):
    upstream_f = upstream.astype(jnp.float32)
    kernel_terms = []
    for offset_row in range(KSIZE):
        for offset_col in range(KSIZE):
            window = padded[offset_row:offset_row + tile_rows, offset_col:offset_col + tile_cols].astype(jnp.float32)
            kernel_terms.append(lax.optimization_barrier(jnp.sum(window * upstream_f, axis=(0, 1))))
    return jnp.stack(kernel_terms)

def normalize(mixed):
    centre = mixed - lax.optimization_barrier(jnp.mean(mixed, axis=-1, keepdims=True))
    variance = lax.optimization_barrier(jnp.mean(centre * centre, axis=-1, keepdims=True))
    inverse = lax.rsqrt(variance + norm_eps)
    return (centre * inverse, inverse)

def split_heads(matrix, head_count):
    return matrix.reshape(matrix.shape[0], head_count, -1).transpose(1, 0, 2)

def merge_heads(stacked):
    return stacked.transpose(1, 0, 2).reshape(stacked.shape[1], -1)

def head_pass(pieces):
    queries, key_rows, values, upstream = pieces
    score_scale = queries.shape[-1] ** (-0.5)
    scores = jnp.dot(queries, key_rows.T, preferred_element_type=jnp.float32) * score_scale
    top_score = lax.optimization_barrier(jnp.max(scores, axis=1, keepdims=True))
    raised = jnp.exp(scores - top_score)
    sum_exp = lax.optimization_barrier(jnp.sum(raised, axis=1, keepdims=True))
    attended = jnp.dot(raised.astype(jnp.bfloat16), values, preferred_element_type=jnp.float32) / sum_exp
    row_dots = lax.optimization_barrier(jnp.sum(upstream.astype(jnp.float32) * attended, axis=1, keepdims=True))
    probs = raised / sum_exp
    d_probs = jnp.dot(upstream, values.T, preferred_element_type=jnp.float32)
    d_scores = (probs * (d_probs - row_dots) * score_scale).astype(jnp.bfloat16)
    q_grad = jnp.dot(d_scores, key_rows, preferred_element_type=jnp.float32)
    k_grad = jnp.dot(d_scores.T, queries, preferred_element_type=jnp.float32).astype(jnp.bfloat16)
    v_grad = jnp.dot(probs.astype(jnp.bfloat16).T, upstream, preferred_element_type=jnp.float32).astype(jnp.bfloat16)
    return (attended, q_grad, k_grad, v_grad)

def reference(pixels, patch_weight, patch_bias, conv_kernel, norm_gain, kv_weight, latents, d_attended):
    tile_rows = pixels.shape[1] // PATCH
    tile_cols = pixels.shape[2] // PATCH
    channels = patch_weight.shape[1]
    model_dim = latents.shape[1]
    patches = patch_rows(pixels)
    embedded = (jnp.dot(patches, patch_weight, preferred_element_type=jnp.float32) + patch_bias).astype(jnp.bfloat16)
    embedded = embedded.reshape(tile_rows, tile_cols, channels)
    half_width = KSIZE // 2
    padded = jnp.pad(embedded, ((half_width, half_width), (half_width, half_width), (0, 0)))
    mixed = embedded.astype(jnp.float32) + depthwise(padded, conv_kernel, tile_rows, tile_cols)
    centred, inverse = normalize(mixed)
    normed = (centred * norm_gain).astype(jnp.bfloat16).reshape(tile_rows * tile_cols, channels)
    projected = jnp.dot(normed, kv_weight, preferred_element_type=jnp.float32).astype(jnp.bfloat16)
    stacked = lax.map(head_pass, (split_heads(latents, HEADS), split_heads(projected[:, :model_dim], HEADS), split_heads(projected[:, model_dim:], HEADS), split_heads(d_attended, HEADS)))
    attended = merge_heads(stacked[0])
    grad_latents = merge_heads(stacked[1])
    d_projected = jnp.concatenate([merge_heads(stacked[2]), merge_heads(stacked[3])], axis=1)
    grad_kv = jnp.dot(normed.T, d_projected, preferred_element_type=jnp.float32)
    d_normed = jnp.dot(d_projected, kv_weight.T, preferred_element_type=jnp.float32).reshape(tile_rows, tile_cols, channels)
    grad_gain = lax.optimization_barrier(jnp.sum(d_normed * centred, axis=(0, 1)))
    scaled = d_normed * norm_gain
    d_mixed = inverse * (scaled - lax.optimization_barrier(jnp.mean(scaled, axis=-1, keepdims=True)) - centred * lax.optimization_barrier(jnp.mean(scaled * centred, axis=-1, keepdims=True)))
    d_mixed = d_mixed.astype(jnp.bfloat16)
    grad_kernel = kernel_grad(padded, d_mixed, tile_rows, tile_cols)
    d_padded = jnp.pad(d_mixed, ((half_width, half_width), (half_width, half_width), (0, 0)))
    d_embedded = (d_mixed.astype(jnp.float32) + transposed(d_padded, conv_kernel, tile_rows, tile_cols)).astype(jnp.bfloat16)
    d_embedded = d_embedded.reshape(tile_rows * tile_cols, channels)
    grad_patch = jnp.dot(patches.T, d_embedded, preferred_element_type=jnp.float32)
    grad_bias = lax.optimization_barrier(jnp.sum(d_embedded.astype(jnp.float32), axis=0))
    return (attended, grad_latents, grad_kv, grad_gain, grad_kernel, grad_patch, grad_bias)
```

```python
import functools

import jax
import jax.numpy as jnp
from jax import lax
from jax.experimental import pallas as pl
from jax.experimental.pallas import tpu as pltpu
from jax.sharding import PartitionSpec as P

PATCH = 4
KSIZE = 7
HEADS = 8
HALF = KSIZE // 2
LANES = 128
GROUP = 8
LOG2E = 1.4426950408889634
VMEM_LIMIT = 56 * 1024 * 1024

norm_eps = 1e-05
f32 = jnp.float32
bf16 = jnp.bfloat16


def padded_2(x, sides, width):
    for axis, dim in sides:
        devices, length = (lax.axis_size(axis), x.shape[dim])
        up = [(i, (i + 1) % devices) for i in range(devices - 1)]
        down = [(j, i) for i, j in up]
        last = lax.slice_in_dim(x, length - width, length, axis=dim)
        leading = lax.slice_in_dim(x, 0, width, axis=dim)
        before = lax.ppermute(last, axis, up)
        after = lax.ppermute(leading, axis, down)
        x = jnp.concatenate([before, x, after], axis=dim)
    return x


def patch_rows(pixels):
    in_channels, height, image_width = pixels.shape
    blocks = pixels.reshape(in_channels, height // PATCH, PATCH, image_width // PATCH, PATCH)
    blocks = blocks.transpose(1, 3, 0, 2, 4)
    return blocks.reshape(height // PATCH * (image_width // PATCH), in_channels * PATCH * PATCH)


def halves(x):
    rows, cols, channels = x.shape
    return x.reshape(rows, cols, channels // LANES, LANES).transpose(2, 0, 1, 3)


def conv_windows(x_ref, w_ref, out_ref, tile_rows, tile_cols, flipped):
    groups = tile_rows // GROUP

    def body(n, carry):
        h = n // groups
        r0 = (n % groups) * GROUP
        for cb in range(tile_cols // 8):
            acc = x_ref[h, pl.ds(r0 + HALF, GROUP), cb * 8 + HALF : cb * 8 + HALF + 8, :].astype(f32)
            for j in range(KSIZE):
                x = x_ref[h, pl.ds(r0, GROUP + KSIZE - 1), cb * 8 + j : cb * 8 + j + 8, :].astype(f32)
                for i in range(KSIZE):
                    tap = i * KSIZE + j
                    if flipped:
                        tap = KSIZE * KSIZE - 1 - tap
                    acc = acc + x[i : i + GROUP] * w_ref[h, tap][None]
            out_ref[h, pl.ds(r0, GROUP), cb * 8 : cb * 8 + 8, :] = acc
        return carry

    lax.fori_loop(0, 2 * groups, body, 0)


def norm_rows(m0, m1):
    channels = 2 * LANES
    mean = (jnp.sum(m0, axis=-1, keepdims=True) + jnp.sum(m1, axis=-1, keepdims=True)) / channels
    c0 = m0 - mean
    c1 = m1 - mean
    variance = (
        jnp.sum(c0 * c0, axis=-1, keepdims=True) + jnp.sum(c1 * c1, axis=-1, keepdims=True)
    ) / channels
    inverse = lax.rsqrt(variance + norm_eps)
    return c0 * inverse, c1 * inverse, inverse


def forward_kernel(
    tile_rows, tile_cols, x_ref, w_ref, gain_ref, kv_ref, qt_ref, dat_ref,
    mixed_ref, proj_ref, stats_ref, weighted_ref, normed, scores,
):
    tokens = tile_rows * tile_cols

    @pl.when(pl.program_id(0) == 0)
    def _():
        conv_windows(x_ref, w_ref, mixed_ref, tile_rows, tile_cols, False)

        def body(a, carry):
            c0, c1, _ = norm_rows(mixed_ref[0, a], mixed_ref[1, a])
            rows = pl.ds(pl.multiple_of(a * tile_cols, tile_cols), tile_cols)
            normed[rows, :LANES] = (c0 * gain_ref[:, :LANES]).astype(bf16)
            normed[rows, LANES:] = (c1 * gain_ref[:, LANES:]).astype(bf16)
            return carry

        lax.fori_loop(0, tile_rows, body, 0)

    chunk = 512
    scale = LOG2E * LANES**-0.5
    peak = jnp.full((1, scores.shape[1]), -jnp.inf, f32)
    for n in range(tokens // chunk):
        rows = slice(n * chunk, (n + 1) * chunk)
        proj = jnp.dot(normed[rows, :], kv_ref[0], preferred_element_type=f32).astype(bf16)
        proj_ref[0, rows, :] = proj
        s = jnp.dot(proj[:, :LANES], qt_ref[0], preferred_element_type=f32) * scale
        scores[rows, :] = s
        peak = jnp.maximum(peak, jnp.max(s, axis=0, keepdims=True))
    total = jnp.zeros_like(peak)
    weighted = jnp.zeros((LANES, scores.shape[1]), f32)
    for n in range(tokens // chunk):
        rows = slice(n * chunk, (n + 1) * chunk)
        raised = jnp.exp2(scores[rows, :] - peak)
        total = total + jnp.sum(raised, axis=0, keepdims=True)
        weighted = weighted + lax.dot_general(
            proj_ref[0, rows, LANES:], raised.astype(bf16), (((0,), (0,)), ((), ())),
            preferred_element_type=f32,
        )
    stats_ref[0, 0] = peak
    stats_ref[1, 0] = total
    stats_ref[2, 0] = jnp.sum(weighted * dat_ref[0].astype(f32), axis=0, keepdims=True)
    weighted_ref[0] = weighted


def backward_kernel(
    tile_rows, tile_cols, mixed_ref, gain_ref, proj_ref, qt_ref, q_ref, dat_ref, da_ref,
    kvt_ref, shift_ref, dots_ref, top_ref, weighted_ref,
    large_ref, d_mixed_ref, grad_gain_ref, normed, d_proj, d_normed,
):
    tokens = tile_rows * tile_cols
    chunk = 512
    scale = LANES**-0.5

    @pl.when(pl.program_id(0) == 0)
    def _():
        def body(a, carry):
            c0, c1, _ = norm_rows(mixed_ref[0, a], mixed_ref[1, a])
            rows = pl.ds(pl.multiple_of(a * tile_cols, tile_cols), tile_cols)
            normed[rows, :LANES] = (c0 * gain_ref[:, :LANES]).astype(bf16)
            normed[rows, LANES:] = (c1 * gain_ref[:, LANES:]).astype(bf16)
            d_normed[rows, :] = jnp.zeros((tile_cols, 2 * LANES), f32)
            return carry

        lax.fori_loop(0, tile_rows, body, 0)

    shift = shift_ref[0]
    dots = dots_ref[0]
    grad_q = jnp.zeros((LANES, shift.shape[1]), f32)
    grad_kv = jnp.zeros((2 * LANES, 2 * LANES), f32)
    for n in range(tokens // chunk):
        rows = slice(n * chunk, (n + 1) * chunk)
        keys = proj_ref[0, rows, :LANES]
        values = proj_ref[0, rows, LANES:]
        s = jnp.dot(keys, qt_ref[0], preferred_element_type=f32) * (LOG2E * scale)
        probs = jnp.exp2(s - shift)
        d_probs = jnp.dot(values, dat_ref[0], preferred_element_type=f32)
        d_scores = (probs * (d_probs - dots)).astype(bf16)
        grad_q = grad_q + lax.dot_general(
            keys, d_scores, (((0,), (0,)), ((), ())), preferred_element_type=f32
        )
        d_keys = jnp.dot(d_scores, q_ref[0], preferred_element_type=f32) * scale
        d_values = jnp.dot(probs.astype(bf16), da_ref[0], preferred_element_type=f32)
        both = jnp.concatenate([d_keys.astype(bf16), d_values.astype(bf16)], axis=1)
        d_normed[rows, :] += jnp.dot(both, kvt_ref[0], preferred_element_type=f32)
        grad_kv = grad_kv + lax.dot_general(
            normed[rows, :], both, (((0,), (0,)), ((), ())), preferred_element_type=f32
        )
    attended = weighted_ref[0] * jnp.exp2(top_ref[0] - shift)
    for n in range(large_ref.shape[1]):
        lanes = slice(n * LANES, (n + 1) * LANES)
        large_ref[0, n, :LANES] = attended[:, lanes].astype(bf16)
        large_ref[0, n, LANES : 2 * LANES] = (grad_q[:, lanes] * scale).astype(bf16)
        large_ref[0, n, 2 * LANES :] = grad_kv[:, lanes].astype(bf16)

    @pl.when(pl.program_id(0) == pl.num_programs(0) - 1)
    def _():
        def body(a, carry):
            gg0, gg1 = carry
            c0, c1, inverse = norm_rows(mixed_ref[0, a], mixed_ref[1, a])
            rows = pl.ds(pl.multiple_of(a * tile_cols, tile_cols), tile_cols)
            d0 = d_normed[rows, :LANES]
            d1 = d_normed[rows, LANES:]
            gg0 = gg0 + jnp.sum(d0 * c0, axis=0, keepdims=True)
            gg1 = gg1 + jnp.sum(d1 * c1, axis=0, keepdims=True)
            s0 = d0 * gain_ref[:, :LANES]
            s1 = d1 * gain_ref[:, LANES:]
            mean = (
                jnp.sum(s0, axis=-1, keepdims=True) + jnp.sum(s1, axis=-1, keepdims=True)
            ) / (2 * LANES)
            dot = (
                jnp.sum(s0 * c0, axis=-1, keepdims=True) + jnp.sum(s1 * c1, axis=-1, keepdims=True)
            ) / (2 * LANES)
            m0 = inverse * (s0 - mean - c0 * dot)
            m1 = inverse * (s1 - mean - c1 * dot)
            d_mixed_ref[0, a] = m0.astype(bf16).astype(f32)
            d_mixed_ref[1, a] = m1.astype(bf16).astype(f32)
            return gg0, gg1

        zero = jnp.zeros((1, LANES), f32)
        gg0, gg1 = lax.fori_loop(0, tile_rows, body, (zero, zero))
        grad_gain_ref[:, :LANES] = gg0
        grad_gain_ref[:, LANES:] = gg1


def kernel_grad_kernel(tile_rows, tile_cols, x_ref, d_ref, out_ref, acc_ref):
    groups = tile_rows // GROUP
    acc_ref[...] = jnp.zeros_like(acc_ref)

    def body(n, carry):
        h = n // groups
        r0 = (n % groups) * GROUP
        for cb in range(tile_cols // 8):
            d = d_ref[h, pl.ds(r0, GROUP), cb * 8 : cb * 8 + 8, :]
            for j in range(KSIZE):
                x = x_ref[h, pl.ds(r0, GROUP + KSIZE - 1), cb * 8 + j : cb * 8 + j + 8, :].astype(f32)
                for i in range(KSIZE):
                    acc_ref[h, i * KSIZE + j] += jnp.sum(x[i : i + GROUP] * d, axis=0)
        return carry

    lax.fori_loop(0, 2 * groups, body, 0)
    out_ref[...] = jnp.sum(acc_ref[...], axis=2)


def transposed_kernel(tile_rows, tile_cols, d_ref, w_ref, patches_ref, patch_ref, bias_ref, out):
    conv_windows(d_ref, w_ref, out, tile_rows, tile_cols, True)
    for h in range(2):
        d = out[h].reshape(tile_rows * tile_cols, LANES).astype(bf16)
        patch_ref[:, h * LANES : (h + 1) * LANES] = jnp.dot(
            patches_ref[...], d, preferred_element_type=f32
        )
        bias_ref[:, h * LANES : (h + 1) * LANES] = jnp.sum(d.astype(f32), axis=0, keepdims=True)


MESH = pl.DeviceIdType.MESH


def greet(row, col, rows, cols):
    barrier = pltpu.get_barrier_semaphore()
    for p in range(1, cols):
        pl.semaphore_signal(
            barrier, inc=1, device_id=(row, lax.rem(col + p, cols)), device_id_type=MESH
        )
    for p in range(1, rows):
        pl.semaphore_signal(
            barrier, inc=1, device_id=(lax.rem(row + p, rows), col), device_id_type=MESH
        )
    pl.semaphore_wait(barrier, rows + cols - 2)


def push(src, dst, sems, stage, slot, device):
    copy = pltpu.make_async_remote_copy(
        src_ref=src,
        dst_ref=dst,
        send_sem=sems.at[0, stage, slot],
        recv_sem=sems.at[1, stage, slot],
        device_id=device,
        device_id_type=MESH,
    )
    copy.start()
    return copy


def await_into(dst, sems, stage, slot, device):
    pltpu.make_async_remote_copy(
        src_ref=dst,
        dst_ref=dst,
        send_sem=sems.at[0, stage, slot],
        recv_sem=sems.at[1, stage, slot],
        device_id=device,
        device_id_type=MESH,
    ).wait_recv()


def spread(out_ref, sems, row, col, rows, cols):
    copies = []
    for p in range(1, rows):
        there = (lax.rem(row + p, rows), col)
        copies.append(push(out_ref.at[col, row], out_ref.at[col, row], sems, 2, p, there))
    for p in range(1, rows):
        source = lax.rem(row + rows - p, rows)
        await_into(out_ref.at[col, source], sems, 2, p, (source, col))
    for p in range(1, cols):
        there = (row, lax.rem(col + p, cols))
        copies.append(push(out_ref.at[col], out_ref.at[col], sems, 3, p, there))
    for p in range(1, cols):
        source = lax.rem(col + cols - p, cols)
        await_into(out_ref.at[source], sems, 3, p, (row, source))
    for copy in copies:
        copy.wait_send()


def sum_kernel(x_ref, out_ref, first, middle, second, sems):
    cols, rows, n, _ = x_ref.shape
    row, col = lax.axis_index("rows"), lax.axis_index("cols")
    greet(row, col, rows, cols)
    copies = []
    for p in range(1, cols):
        there = lax.rem(col + p, cols)
        copies.append(push(x_ref.at[there], first.at[p], sems, 0, p, (row, there)))
    for p in range(1, cols):
        await_into(first.at[p], sems, 0, p, (row, lax.rem(col + cols - p, cols)))

    def body(r, carry):
        acc = x_ref[col, r].astype(f32)
        for p in range(1, cols):
            acc = acc + first[p, r].astype(f32)
        middle[r] = acc.astype(middle.dtype)
        return carry

    lax.fori_loop(0, rows, body, 0)
    for p in range(1, rows):
        there = lax.rem(row + p, rows)
        copies.append(push(middle.at[there], second.at[p], sems, 1, p, (there, col)))
    for p in range(1, rows):
        await_into(second.at[p], sems, 1, p, (lax.rem(row + rows - p, rows), col))
    acc = middle[row].astype(f32)
    for p in range(1, rows):
        acc = acc + second[p].astype(f32)
    out_ref[col, row] = acc.astype(out_ref.dtype)
    spread(out_ref, sems, row, col, rows, cols)
    for copy in copies:
        copy.wait_send()


def reduced(x, rows, cols, collective_id):
    count = x.shape[0]
    unit = rows * cols * (16 if x.dtype == bf16 else 8)
    padded = pl.cdiv(count, unit) * unit
    n = padded // (rows * cols)
    x = jnp.pad(x, ((0, padded - count), (0, 0))).reshape(cols, rows, n, LANES)
    vmem = pl.BlockSpec(memory_space=pltpu.VMEM)
    out = pl.pallas_call(
        sum_kernel,
        out_shape=jax.ShapeDtypeStruct(x.shape, x.dtype),
        in_specs=[vmem],
        out_specs=vmem,
        scratch_shapes=[
            pltpu.VMEM((cols, rows, n, LANES), x.dtype),
            pltpu.VMEM((rows, n, LANES), x.dtype),
            pltpu.VMEM((rows, n, LANES), x.dtype),
            pltpu.SemaphoreType.DMA((2, 4, max(rows, cols))),
        ],
        compiler_params=pltpu.CompilerParams(
            collective_id=collective_id, has_side_effects=True, vmem_limit_bytes=VMEM_LIMIT
        ),
        name="reduce" + str(collective_id),
    )(x)
    return out.reshape(padded, LANES)[:count]


def combine(stats):
    peak = jnp.max(stats[:, 0], axis=0)
    factor = jnp.exp2(stats[:, 0] - peak[None])
    return jnp.stack(
        [peak, jnp.sum(stats[:, 1] * factor, axis=0), jnp.sum(stats[:, 2] * factor, axis=0)]
    )


def stats_kernel(rows, cols, x_ref, out_ref, first, second, sems):
    row, col = lax.axis_index("rows"), lax.axis_index("cols")
    greet(row, col, rows, cols)
    copies = []
    first[0] = x_ref[...]
    for p in range(1, cols):
        there = (row, lax.rem(col + p, cols))
        copies.append(push(x_ref, first.at[p], sems, 0, p, there))
    for p in range(1, cols):
        await_into(first.at[p], sems, 0, p, (row, lax.rem(col + cols - p, cols)))
    second[0] = combine(first[...])
    for p in range(1, rows):
        there = (lax.rem(row + p, rows), col)
        copies.append(push(second.at[0], second.at[p], sems, 1, p, there))
    for p in range(1, rows):
        await_into(second.at[p], sems, 1, p, (lax.rem(row + rows - p, rows), col))
    total = combine(second[...])
    out_ref[0] = total[0] + jnp.log2(total[1])
    out_ref[1] = total[2] / total[1]
    for copy in copies:
        copy.wait_send()


def mesh_stats(x, rows, cols):
    vmem = pl.BlockSpec(memory_space=pltpu.VMEM)
    return pl.pallas_call(
        functools.partial(stats_kernel, rows, cols),
        out_shape=struct(2, *x.shape[1:]),
        in_specs=[vmem],
        out_specs=vmem,
        scratch_shapes=[
            pltpu.VMEM((cols,) + x.shape, f32),
            pltpu.VMEM((rows,) + x.shape, f32),
            pltpu.SemaphoreType.DMA((2, 2, max(rows, cols))),
        ],
        compiler_params=pltpu.CompilerParams(
            collective_id=1, has_side_effects=True, vmem_limit_bytes=VMEM_LIMIT
        ),
        name="stats",
    )(x)


def head_spec(shape):
    return pl.BlockSpec((1,) + shape, lambda n: (n, 0, 0))


def whole_spec(shape):
    return pl.BlockSpec(shape, lambda n: (0,) * len(shape))


def struct(*shape, dtype=f32):
    return jax.ShapeDtypeStruct(shape, dtype)


def per_device(
    pixels, patch_weight, patch_bias, conv_kernel, norm_gain, kv_weight, latents, d_attended
):
    tile_rows = pixels.shape[1] // PATCH
    tile_cols = pixels.shape[2] // PATCH
    tokens = tile_rows * tile_cols
    channels = patch_weight.shape[1]
    count, model_dim = latents.shape
    parts = count // LANES
    patches = patch_rows(pixels)
    embedded = (
        jnp.dot(patches, patch_weight, preferred_element_type=f32) + patch_bias
    ).astype(bf16)
    embedded = embedded.reshape(tile_rows, tile_cols, channels)
    sides = (("rows", 0), ("cols", 1))
    pad_rows, pad_cols = tile_rows + 2 * HALF, tile_cols + 8

    def windows(x):
        x = padded_2(x, sides, HALF)
        x = jnp.pad(x, ((0, 0), (0, 8 - 2 * HALF), (0, 0)))
        return halves(x).astype(f32)

    taps = KSIZE * KSIZE
    taps_w = conv_kernel.reshape(taps, 2, LANES).transpose(1, 0, 2)
    taps_w = jnp.broadcast_to(taps_w[:, :, None, :], (2, taps, 8, LANES))
    gain = norm_gain.reshape(1, channels)
    kv = kv_weight.reshape(channels, 2, HEADS, LANES).transpose(2, 0, 1, 3)
    kv = kv.reshape(HEADS, channels, 2 * LANES)
    kvt = kv.transpose(0, 2, 1)
    q = latents.reshape(count, HEADS, LANES).transpose(1, 0, 2)
    qt = q.transpose(0, 2, 1)
    da = d_attended.reshape(count, HEADS, LANES).transpose(1, 0, 2)
    dat = da.transpose(0, 2, 1)
    x = windows(embedded)
    params = pltpu.CompilerParams(vmem_limit_bytes=VMEM_LIMIT)
    mixed, proj, stats, weighted = pl.pallas_call(
        functools.partial(forward_kernel, tile_rows, tile_cols),
        grid=(HEADS,),
        in_specs=[
            whole_spec((2, pad_rows, pad_cols, LANES)),
            whole_spec((2, taps, 8, LANES)),
            whole_spec((1, channels)),
            head_spec((channels, 2 * LANES)),
            head_spec((LANES, count)),
            head_spec((LANES, count)),
        ],
        out_specs=[
            whole_spec((2, tile_rows, tile_cols, LANES)),
            head_spec((tokens, 2 * LANES)),
            pl.BlockSpec((3, 1, 1, count), lambda n: (0, n, 0, 0)),
            head_spec((LANES, count)),
        ],
        out_shape=[
            struct(2, tile_rows, tile_cols, LANES),
            struct(HEADS, tokens, 2 * LANES, dtype=bf16),
            struct(3, HEADS, 1, count),
            struct(HEADS, LANES, count),
        ],
        scratch_shapes=[pltpu.VMEM((tokens, channels), bf16), pltpu.VMEM((tokens, count), f32)],
        compiler_params=params,
        name="forward",
    )(x, taps_w, gain, kv, qt, dat)
    rows, cols = lax.axis_size("rows"), lax.axis_size("cols")
    shared = mesh_stats(stats.reshape(3, HEADS, count), rows, cols)
    shift, dots = shared.reshape(2, HEADS, 1, count)
    tops = stats[0]
    large, d_mixed, grad_gain = pl.pallas_call(
        functools.partial(backward_kernel, tile_rows, tile_cols),
        grid=(HEADS,),
        in_specs=[
            whole_spec((2, tile_rows, tile_cols, LANES)),
            whole_spec((1, channels)),
            head_spec((tokens, 2 * LANES)),
            head_spec((LANES, count)),
            head_spec((count, LANES)),
            head_spec((LANES, count)),
            head_spec((count, LANES)),
            head_spec((2 * LANES, channels)),
            head_spec((1, count)),
            head_spec((1, count)),
            head_spec((1, count)),
            head_spec((LANES, count)),
        ],
        out_specs=[
            pl.BlockSpec((1, parts, 4 * LANES, LANES), lambda n: (n, 0, 0, 0)),
            whole_spec((2, tile_rows, tile_cols, LANES)),
            whole_spec((1, channels)),
        ],
        out_shape=[
            struct(HEADS, parts, 4 * LANES, LANES, dtype=bf16),
            struct(2, tile_rows, tile_cols, LANES),
            struct(1, channels),
        ],
        scratch_shapes=[
            pltpu.VMEM((tokens, channels), bf16),
            pltpu.VMEM((8, LANES), bf16),
            pltpu.VMEM((tokens, channels), f32),
        ],
        compiler_params=params,
        name="backward",
    )(mixed, gain, proj, qt, q, dat, da, kvt, shift, dots, tops, weighted)
    large = reduced(large.reshape(-1, LANES), rows, cols, 2).astype(f32)
    large = large.reshape(HEADS, parts, 4 * LANES, LANES)
    d_tile = d_mixed.transpose(1, 2, 0, 3).reshape(tile_rows, tile_cols, channels).astype(bf16)
    d_padded = windows(d_tile)
    grad_kernel = pl.pallas_call(
        functools.partial(kernel_grad_kernel, tile_rows, tile_cols),
        out_shape=struct(2, taps, LANES),
        scratch_shapes=[pltpu.VMEM((2, taps, 8, LANES), f32)],
        compiler_params=params,
        name="kernel_grad",
    )(x, d_mixed)
    grad_patch, grad_bias = pl.pallas_call(
        functools.partial(transposed_kernel, tile_rows, tile_cols),
        out_shape=[struct(patches.shape[1], channels), struct(1, channels)],
        scratch_shapes=[pltpu.VMEM((2, tile_rows, tile_cols, LANES), f32)],
        compiler_params=params,
        name="transposed",
    )(d_padded, taps_w, patches.T)
    small = jnp.concatenate(
        [grad_kernel.transpose(1, 0, 2).reshape(taps, channels), grad_gain, grad_patch, grad_bias]
    )
    small = reduced(small.reshape(-1, LANES), rows, cols, 3).reshape(small.shape)
    attended = large[:, :, :LANES].transpose(1, 3, 0, 2).reshape(count, model_dim)
    grad_latents = large[:, :, LANES : 2 * LANES].transpose(1, 3, 0, 2).reshape(count, model_dim)
    grad_kv = large[:, :, 2 * LANES :].transpose(2, 1, 0, 3).reshape(channels, 2 * model_dim)
    return (
        attended,
        grad_latents,
        grad_kv,
        small[taps],
        small[:taps],
        small[taps + 1 : -1],
        small[-1],
    )


def solution(mesh):
    return jax.shard_map(
        per_device,
        mesh=mesh,
        in_specs=(P(None, "rows", "cols"), P(), P(), P(), P(), P(), P(), P()),
        out_specs=(P(), P(), P(), P(), P(), P(), P()),
        check_vma=False,
    )
```

```python
import functools

import jax
import jax.numpy as jnp
from jax import lax
from jax.experimental import pallas as pl
from jax.experimental.pallas import tpu as pltpu
from jax.sharding import PartitionSpec as P

PATCH = 4
KSIZE = 7
HEADS = 8
HALF = KSIZE // 2
EDGE = 8 - HALF
LANES = 128
GROUP = 8
LOG2E = 1.4426950408889634
VMEM_LIMIT = 56 * 1024 * 1024

norm_eps = 1e-05
f32 = jnp.float32
bf16 = jnp.bfloat16


def patch_columns(pixels):
    fields, height, width = pixels.shape
    place = jnp.arange(width)
    target = (place % PATCH) * (width // PATCH) + place // PATCH
    sort = (target[:, None] == place[None, :]).astype(bf16)
    x = jnp.dot(pixels.reshape(fields * height, width), sort, preferred_element_type=f32)
    x = x.astype(bf16).reshape(fields, height // PATCH, PATCH, PATCH, width // PATCH)
    x = x.transpose(0, 2, 3, 1, 4)
    return x.reshape(fields * PATCH * PATCH, height // PATCH * (width // PATCH))


def conv_windows(x_ref, w_ref, out_ref, tile_rows, tile_cols, flipped, part=None):
    groups = tile_rows // GROUP
    first, last = (0, 2 * groups) if part is None else (part * groups, (part + 1) * groups)

    def body(n, carry):
        h = n // groups
        r0 = (n % groups) * GROUP
        for cb in range(tile_cols // 8):
            acc = x_ref[h, pl.ds(r0 + HALF, GROUP), cb * 8 + 8 : cb * 8 + 16, :].astype(f32)
            for j in range(KSIZE):
                x = x_ref[h, pl.ds(r0, GROUP + KSIZE - 1), cb * 8 + EDGE + j : cb * 8 + EDGE + j + 8, :].astype(f32)
                for i in range(KSIZE):
                    tap = i * KSIZE + j
                    if flipped:
                        tap = KSIZE * KSIZE - 1 - tap
                    acc = acc + x[i : i + GROUP] * w_ref[h, tap][None]
            out_ref[h, pl.ds(r0, GROUP), cb * 8 : cb * 8 + 8, :] = acc
        return carry

    lax.fori_loop(first, last, body, 0)


def norm_rows(m0, m1):
    channels = 2 * LANES
    mean = (jnp.sum(m0, axis=-1, keepdims=True) + jnp.sum(m1, axis=-1, keepdims=True)) / channels
    c0 = m0 - mean
    c1 = m1 - mean
    variance = (
        jnp.sum(c0 * c0, axis=-1, keepdims=True) + jnp.sum(c1 * c1, axis=-1, keepdims=True)
    ) / channels
    inverse = lax.rsqrt(variance + norm_eps)
    return c0 * inverse, c1 * inverse, inverse


def forward_kernel(
    tile_rows, tile_cols, x_ref, w_ref, gain_ref, kv_ref, qt_ref, dat_ref,
    mixed_ref, proj_ref, stats_ref, weighted_ref, normed, scores,
):
    tokens = tile_rows * tile_cols

    @pl.when(pl.program_id(0) == 0)
    def _():
        conv_windows(x_ref, w_ref, mixed_ref, tile_rows, tile_cols, False)

        def body(a, carry):
            c0, c1, _ = norm_rows(mixed_ref[0, a], mixed_ref[1, a])
            rows = pl.ds(pl.multiple_of(a * tile_cols, tile_cols), tile_cols)
            normed[rows, :LANES] = (c0 * gain_ref[:, :LANES]).astype(bf16)
            normed[rows, LANES:] = (c1 * gain_ref[:, LANES:]).astype(bf16)
            return carry

        lax.fori_loop(0, tile_rows, body, 0)

    chunk = 512
    scale = LOG2E * LANES**-0.5
    peak = jnp.full((1, scores.shape[1]), -jnp.inf, f32)
    for n in range(tokens // chunk):
        rows = slice(n * chunk, (n + 1) * chunk)
        proj = jnp.dot(normed[rows, :], kv_ref[0], preferred_element_type=f32).astype(bf16)
        proj_ref[0, rows, :] = proj
        s = jnp.dot(proj[:, :LANES], qt_ref[0], preferred_element_type=f32) * scale
        scores[rows, :] = s
        peak = jnp.maximum(peak, jnp.max(s, axis=0, keepdims=True))
    total = jnp.zeros_like(peak)
    weighted = jnp.zeros((LANES, scores.shape[1]), f32)
    for n in range(tokens // chunk):
        rows = slice(n * chunk, (n + 1) * chunk)
        raised = jnp.exp2(scores[rows, :] - peak)
        total = total + jnp.sum(raised, axis=0, keepdims=True)
        weighted = weighted + lax.dot_general(
            proj_ref[0, rows, LANES:], raised.astype(bf16), (((0,), (0,)), ((), ())),
            preferred_element_type=f32,
        )
    stats_ref[0, 0] = peak
    stats_ref[1, 0] = total
    stats_ref[2, 0] = jnp.sum(weighted * dat_ref[0].astype(f32), axis=0, keepdims=True)
    weighted_ref[0] = weighted


def backward_kernel(
    tile_rows, tile_cols, mixed_ref, gain_ref, proj_ref, qt_ref, q_ref, dat_ref, da_ref,
    kvt_ref, shift_ref, dots_ref, top_ref, weighted_ref,
    large_ref, d_mixed_ref, grad_gain_ref, normed, d_proj, d_normed,
):
    tokens = tile_rows * tile_cols
    chunk = 512
    scale = LANES**-0.5

    @pl.when(pl.program_id(0) == 0)
    def _():
        def body(a, carry):
            c0, c1, _ = norm_rows(mixed_ref[0, a], mixed_ref[1, a])
            rows = pl.ds(pl.multiple_of(a * tile_cols, tile_cols), tile_cols)
            normed[rows, :LANES] = (c0 * gain_ref[:, :LANES]).astype(bf16)
            normed[rows, LANES:] = (c1 * gain_ref[:, LANES:]).astype(bf16)
            d_normed[rows, :] = jnp.zeros((tile_cols, 2 * LANES), f32)
            return carry

        lax.fori_loop(0, tile_rows, body, 0)

    shift = shift_ref[0]
    dots = dots_ref[0]
    grad_q = jnp.zeros((LANES, shift.shape[1]), f32)
    grad_kv = jnp.zeros((2 * LANES, 2 * LANES), f32)
    for n in range(tokens // chunk):
        rows = slice(n * chunk, (n + 1) * chunk)
        keys = proj_ref[0, rows, :LANES]
        values = proj_ref[0, rows, LANES:]
        s = jnp.dot(keys, qt_ref[0], preferred_element_type=f32) * (LOG2E * scale)
        probs = jnp.exp2(s - shift)
        d_probs = jnp.dot(values, dat_ref[0], preferred_element_type=f32)
        d_scores = (probs * (d_probs - dots)).astype(bf16)
        grad_q = grad_q + lax.dot_general(
            keys, d_scores, (((0,), (0,)), ((), ())), preferred_element_type=f32
        )
        d_keys = jnp.dot(d_scores, q_ref[0], preferred_element_type=f32) * scale
        d_values = jnp.dot(probs.astype(bf16), da_ref[0], preferred_element_type=f32)
        both = jnp.concatenate([d_keys.astype(bf16), d_values.astype(bf16)], axis=1)
        d_normed[rows, :] += jnp.dot(both, kvt_ref[0], preferred_element_type=f32)
        grad_kv = grad_kv + lax.dot_general(
            normed[rows, :], both, (((0,), (0,)), ((), ())), preferred_element_type=f32
        )
    attended = weighted_ref[0] * jnp.exp2(top_ref[0] - shift)
    for n in range(large_ref.shape[1]):
        lanes = slice(n * LANES, (n + 1) * LANES)
        large_ref[0, n, :LANES] = attended[:, lanes].astype(bf16)
        large_ref[0, n, LANES : 2 * LANES] = (grad_q[:, lanes] * scale).astype(bf16)
        large_ref[0, n, 2 * LANES :] = grad_kv[:, lanes].astype(bf16)

    @pl.when(pl.program_id(0) == pl.num_programs(0) - 1)
    def _():
        def body(a, carry):
            gg0, gg1 = carry
            c0, c1, inverse = norm_rows(mixed_ref[0, a], mixed_ref[1, a])
            rows = pl.ds(pl.multiple_of(a * tile_cols, tile_cols), tile_cols)
            d0 = d_normed[rows, :LANES]
            d1 = d_normed[rows, LANES:]
            gg0 = gg0 + jnp.sum(d0 * c0, axis=0, keepdims=True)
            gg1 = gg1 + jnp.sum(d1 * c1, axis=0, keepdims=True)
            s0 = d0 * gain_ref[:, :LANES]
            s1 = d1 * gain_ref[:, LANES:]
            mean = (
                jnp.sum(s0, axis=-1, keepdims=True) + jnp.sum(s1, axis=-1, keepdims=True)
            ) / (2 * LANES)
            dot = (
                jnp.sum(s0 * c0, axis=-1, keepdims=True) + jnp.sum(s1 * c1, axis=-1, keepdims=True)
            ) / (2 * LANES)
            m0 = inverse * (s0 - mean - c0 * dot)
            m1 = inverse * (s1 - mean - c1 * dot)
            d_mixed_ref[0, a] = m0.astype(bf16).astype(f32)
            d_mixed_ref[1, a] = m1.astype(bf16).astype(f32)
            return gg0, gg1

        zero = jnp.zeros((1, LANES), f32)
        gg0, gg1 = lax.fori_loop(0, tile_rows, body, (zero, zero))
        grad_gain_ref[:, :LANES] = gg0
        grad_gain_ref[:, LANES:] = gg1


def kernel_grad(x_ref, d_ref, acc_ref, tile_rows, tile_cols, h):
    acc_ref[h] = jnp.zeros(acc_ref.shape[1:], f32)

    def body(n, carry):
        r0 = n * GROUP
        for cb in range(tile_cols // 8):
            d = d_ref[h, pl.ds(r0 + HALF, GROUP), cb * 8 + 8 : cb * 8 + 16, :]
            for j in range(KSIZE):
                lanes = slice(cb * 8 + EDGE + j, cb * 8 + EDGE + j + 8)
                x = x_ref[h, pl.ds(r0, GROUP + KSIZE - 1), lanes, :]
                for i in range(KSIZE):
                    acc_ref[h, i * KSIZE + j] += jnp.sum(x[i : i + GROUP] * d, axis=0)
        return carry

    lax.fori_loop(0, tile_rows // GROUP, body, 0)


MESH = pl.DeviceIdType.MESH


def greet(row, col, rows, cols):
    barrier = pltpu.get_barrier_semaphore()
    for p in range(1, cols):
        pl.semaphore_signal(
            barrier, inc=1, device_id=(row, lax.rem(col + p, cols)), device_id_type=MESH
        )
    for p in range(1, rows):
        pl.semaphore_signal(
            barrier, inc=1, device_id=(lax.rem(row + p, rows), col), device_id_type=MESH
        )
    pl.semaphore_wait(barrier, rows + cols - 2)


def push(src, dst, sems, stage, slot, device):
    copy = pltpu.make_async_remote_copy(
        src_ref=src,
        dst_ref=dst,
        send_sem=sems.at[0, stage, slot],
        recv_sem=sems.at[1, stage, slot],
        device_id=device,
        device_id_type=MESH,
    )
    copy.start()
    return copy


def await_into(dst, sems, stage, slot, device):
    pltpu.make_async_remote_copy(
        src_ref=dst,
        dst_ref=dst,
        send_sem=sems.at[0, stage, slot],
        recv_sem=sems.at[1, stage, slot],
        device_id=device,
        device_id_type=MESH,
    ).wait_recv()


def halo_cols(buf, sems, row, col, cols, tile_rows, tile_cols):
    inner = pl.ds(HALF, tile_rows)

    def part(start):
        return buf.at[:, inner, pl.ds(start, 8), :]

    def copies():
        right = pltpu.make_async_remote_copy(
            src_ref=part(tile_cols), dst_ref=part(0), send_sem=sems.at[0, 0], recv_sem=sems.at[1, 0],
            device_id=(row, lax.min(col + 1, cols - 1)), device_id_type=MESH,
        )
        left = pltpu.make_async_remote_copy(
            src_ref=part(8), dst_ref=part(tile_cols + 8), send_sem=sems.at[0, 1], recv_sem=sems.at[1, 1],
            device_id=(row, lax.max(col - 1, 0)), device_id_type=MESH,
        )
        return right, left

    return run_halo(copies, col, cols)


def halo_rows(buf, sems, row, col, rows, tile_rows):
    def part(start):
        return buf.at[:, pl.ds(start, HALF), :, :]

    def copies():
        down = pltpu.make_async_remote_copy(
            src_ref=part(tile_rows), dst_ref=part(0), send_sem=sems.at[0, 2], recv_sem=sems.at[1, 2],
            device_id=(lax.min(row + 1, rows - 1), col), device_id_type=MESH,
        )
        up = pltpu.make_async_remote_copy(
            src_ref=part(HALF), dst_ref=part(tile_rows + HALF), send_sem=sems.at[0, 3], recv_sem=sems.at[1, 3],
            device_id=(lax.max(row - 1, 0), col), device_id_type=MESH,
        )
        return down, up

    return run_halo(copies, row, rows)


def run_halo(copies, me, devices):
    @pl.when(me < devices - 1)
    def _():
        copies()[0].start()

    @pl.when(me > 0)
    def _():
        copies()[1].start()

    def wait():
        @pl.when(me > 0)
        def _():
            copies()[0].wait_recv()
            copies()[1].wait_send()

        @pl.when(me < devices - 1)
        def _():
            copies()[1].wait_recv()
            copies()[0].wait_send()

    return wait


class Reduction:
    def __init__(self, x, out, first, middle, second, sems):
        self.x, self.out, self.first, self.middle, self.second = x, out, first, middle, second
        self.sems = sems
        self.cols, self.rows = x.shape[:2]
        self.row, self.col = lax.axis_index("rows"), lax.axis_index("cols")
        self.copies = []

    def across(self, p):
        return lax.rem(self.col + p, self.cols)

    def along(self, p):
        return lax.rem(self.row + p, self.rows)

    def send_0(self):
        for p in range(1, self.cols):
            there = self.across(p)
            self.copies.append(
                push(self.x.at[there], self.first.at[p], self.sems, 0, p, (self.row, there))
            )

    def sum_0(self):
        for p in range(1, self.cols):
            source = (self.row, self.across(self.cols - p))
            await_into(self.first.at[p], self.sems, 0, p, source)

        def body(r, carry):
            acc = self.x[self.col, r].astype(f32)
            for p in range(1, self.cols):
                acc = acc + self.first[p, r].astype(f32)
            self.middle[r] = acc.astype(self.middle.dtype)
            return carry

        lax.fori_loop(0, self.rows, body, 0)
        for p in range(1, self.rows):
            there = self.along(p)
            self.copies.append(
                push(self.middle.at[there], self.second.at[p], self.sems, 1, p, (there, self.col))
            )

    def sum_1(self):
        for p in range(1, self.rows):
            source = (self.along(self.rows - p), self.col)
            await_into(self.second.at[p], self.sems, 1, p, source)
        acc = self.middle[self.row].astype(f32)
        for p in range(1, self.rows):
            acc = acc + self.second[p].astype(f32)
        self.out[self.col, self.row] = acc.astype(self.out.dtype)
        piece = self.out.at[self.col, self.row]
        for p in range(1, self.rows):
            self.copies.append(push(piece, piece, self.sems, 2, p, (self.along(p), self.col)))

    def spread_2(self):
        for p in range(1, self.rows):
            source = self.along(self.rows - p)
            await_into(self.out.at[self.col, source], self.sems, 2, p, (source, self.col))
        slab = self.out.at[self.col]
        for p in range(1, self.cols):
            self.copies.append(push(slab, slab, self.sems, 3, p, (self.row, self.across(p))))

    def spread_3(self):
        for p in range(1, self.cols):
            source = self.across(self.cols - p)
            await_into(self.out.at[source], self.sems, 3, p, (self.row, source))
        for copy in self.copies:
            copy.wait_send()


def embed_kernel(rows, cols, tile_rows, tile_cols, patches_ref, w_ref, bias_ref, out_ref, buf, sems):
    row, col = lax.axis_index("rows"), lax.axis_index("cols")
    embedded = lax.dot_general(
        patches_ref[...], w_ref[...], (((0,), (0,)), ((), ())), preferred_element_type=f32
    )
    embedded = (embedded + bias_ref[...]).astype(bf16).astype(f32)
    buf[...] = jnp.zeros_like(buf)
    for h in range(2):
        tile = embedded[:, h * LANES : (h + 1) * LANES].reshape(tile_rows, tile_cols, LANES)
        buf[h, HALF : HALF + tile_rows, 8 : 8 + tile_cols, :] = tile
    greet(row, col, rows, cols)
    halo_cols(buf, sems, row, col, cols, tile_rows, tile_cols)()
    halo_rows(buf, sems, row, col, rows, tile_rows)()
    out_ref[...] = buf[...]


def closing_kernel(
    tile_rows, tile_cols, large_ref, x_ref, d_ref, w_ref, patches_ref, gain_ref,
    large_out, small_out,
    buf, acc, out, flat, small, first, middle, second, s_first, s_middle, s_second,
    halo_sems, sems, s_sems,
):
    cols, rows = large_ref.shape[:2]
    row, col = lax.axis_index("rows"), lax.axis_index("cols")
    taps = KSIZE * KSIZE
    buf[...] = jnp.zeros_like(buf)
    buf[:, HALF : HALF + tile_rows, 8 : 8 + tile_cols, :] = d_ref[...]
    flat[...] = jnp.zeros_like(flat)
    greet(row, col, rows, cols)
    big = Reduction(large_ref, large_out, first, middle, second, sems)
    little = Reduction(small, small_out, s_first, s_middle, s_second, s_sems)
    wait = halo_cols(buf, halo_sems, row, col, cols, tile_rows, tile_cols)
    big.send_0()
    kernel_grad(x_ref, d_ref=buf, acc_ref=acc, tile_rows=tile_rows, tile_cols=tile_cols, h=0)
    wait()
    wait = halo_rows(buf, halo_sems, row, col, rows, tile_rows)
    kernel_grad(x_ref, d_ref=buf, acc_ref=acc, tile_rows=tile_rows, tile_cols=tile_cols, h=1)
    wait()
    patch_size = patches_ref.shape[0]
    part = flat.shape[0] // 2
    for h in range(2):
        conv_windows(buf, w_ref, out, tile_rows, tile_cols, True, h)
        d = out[h].reshape(tile_rows * tile_cols, LANES).astype(bf16)
        base = h * part
        flat[base : base + patch_size, :] = jnp.dot(
            patches_ref[...], d, preferred_element_type=f32
        )
        flat[base + patch_size : base + patch_size + taps, :] = jnp.sum(acc[h], axis=1)
        flat[base + part - 2 : base + part - 1, :] = jnp.sum(d.astype(f32), axis=0, keepdims=True)
        flat[base + part - 1 : base + part, :] = gain_ref[:, h * LANES : (h + 1) * LANES]
        if h == 0:
            big.sum_0()
    for n in range(cols * rows):
        block = small.shape[2]
        small[n // rows, n % rows] = flat[n * block : (n + 1) * block, :]
    little.send_0()
    big.sum_1()
    little.sum_0()
    big.spread_2()
    little.sum_1()
    little.spread_2()
    little.spread_3()
    big.spread_3()


def closing(large, x, d_mixed, taps_w, patches_t, grad_gain, rows, cols):
    _, tile_rows, tile_cols, _ = d_mixed.shape
    n = large.size // (rows * cols * LANES)
    large = large.reshape(cols, rows, n, LANES)
    pieces = rows * cols
    needed = 2 * (patches_t.shape[0] + KSIZE * KSIZE + 2)
    m = pl.cdiv(needed, pieces * 8) * 8
    vmem = pl.BlockSpec(memory_space=pltpu.VMEM)
    return pl.pallas_call(
        functools.partial(closing_kernel, tile_rows, tile_cols),
        out_shape=[struct(cols, rows, n, LANES, dtype=bf16), struct(cols, rows, m, LANES)],
        in_specs=[vmem] * 6,
        out_specs=[vmem] * 2,
        scratch_shapes=[
            pltpu.VMEM((2, tile_rows + 2 * HALF, tile_cols + 16, LANES), f32),
            pltpu.VMEM((2, KSIZE * KSIZE, 8, LANES), f32),
            pltpu.VMEM((2, tile_rows, tile_cols, LANES), f32),
            pltpu.VMEM((pieces * m, LANES), f32),
            pltpu.VMEM((cols, rows, m, LANES), f32),
            pltpu.VMEM((cols, rows, n, LANES), bf16),
            pltpu.VMEM((rows, n, LANES), bf16),
            pltpu.VMEM((rows, n, LANES), bf16),
            pltpu.VMEM((cols, rows, m, LANES), f32),
            pltpu.VMEM((rows, m, LANES), f32),
            pltpu.VMEM((rows, m, LANES), f32),
            pltpu.SemaphoreType.DMA((2, 4)),
            pltpu.SemaphoreType.DMA((2, 4, max(rows, cols))),
            pltpu.SemaphoreType.DMA((2, 4, max(rows, cols))),
        ],
        compiler_params=pltpu.CompilerParams(
            collective_id=2, has_side_effects=True, vmem_limit_bytes=VMEM_LIMIT
        ),
        name="closing",
    )(large, x, d_mixed, taps_w, patches_t, grad_gain)


def combine(stats):
    peak = jnp.max(stats[:, 0], axis=0)
    factor = jnp.exp2(stats[:, 0] - peak[None])
    return jnp.stack(
        [peak, jnp.sum(stats[:, 1] * factor, axis=0), jnp.sum(stats[:, 2] * factor, axis=0)]
    )


def stats_kernel(rows, cols, x_ref, out_ref, first, second, sems):
    row, col = lax.axis_index("rows"), lax.axis_index("cols")
    greet(row, col, rows, cols)
    copies = []
    first[0] = x_ref[...]
    for p in range(1, cols):
        there = (row, lax.rem(col + p, cols))
        copies.append(push(x_ref, first.at[p], sems, 0, p, there))
    for p in range(1, cols):
        await_into(first.at[p], sems, 0, p, (row, lax.rem(col + cols - p, cols)))
    second[0] = combine(first[...])
    for p in range(1, rows):
        there = (lax.rem(row + p, rows), col)
        copies.append(push(second.at[0], second.at[p], sems, 1, p, there))
    for p in range(1, rows):
        await_into(second.at[p], sems, 1, p, (lax.rem(row + rows - p, rows), col))
    total = combine(second[...])
    out_ref[0] = total[0] + jnp.log2(total[1])
    out_ref[1] = total[2] / total[1]
    for copy in copies:
        copy.wait_send()


def mesh_stats(x, rows, cols):
    vmem = pl.BlockSpec(memory_space=pltpu.VMEM)
    return pl.pallas_call(
        functools.partial(stats_kernel, rows, cols),
        out_shape=struct(2, *x.shape[1:]),
        in_specs=[vmem],
        out_specs=vmem,
        scratch_shapes=[
            pltpu.VMEM((cols,) + x.shape, f32),
            pltpu.VMEM((rows,) + x.shape, f32),
            pltpu.SemaphoreType.DMA((2, 2, max(rows, cols))),
        ],
        compiler_params=pltpu.CompilerParams(
            collective_id=1, has_side_effects=True, vmem_limit_bytes=VMEM_LIMIT
        ),
        name="stats",
    )(x)


def head_spec(shape):
    return pl.BlockSpec((1,) + shape, lambda n: (n, 0, 0))


def whole_spec(shape):
    return pl.BlockSpec(shape, lambda n: (0,) * len(shape))


def struct(*shape, dtype=f32):
    return jax.ShapeDtypeStruct(shape, dtype)


def per_device(
    pixels, patch_weight, patch_bias, conv_kernel, norm_gain, kv_weight, latents, d_attended
):
    tile_rows = pixels.shape[1] // PATCH
    tile_cols = pixels.shape[2] // PATCH
    tokens = tile_rows * tile_cols
    channels = patch_weight.shape[1]
    count, model_dim = latents.shape
    parts = count // LANES
    rows, cols = lax.axis_size("rows"), lax.axis_size("cols")
    patches_t = patch_columns(pixels)
    pad_rows, pad_cols = tile_rows + 2 * HALF, tile_cols + 16
    vmem = pl.BlockSpec(memory_space=pltpu.VMEM)
    x = pl.pallas_call(
        functools.partial(embed_kernel, rows, cols, tile_rows, tile_cols),
        out_shape=struct(2, pad_rows, pad_cols, LANES),
        in_specs=[vmem] * 3,
        out_specs=vmem,
        scratch_shapes=[
            pltpu.VMEM((2, pad_rows, pad_cols, LANES), f32),
            pltpu.SemaphoreType.DMA((2, 4)),
        ],
        compiler_params=pltpu.CompilerParams(
            collective_id=3, has_side_effects=True, vmem_limit_bytes=VMEM_LIMIT
        ),
        name="embed",
    )(patches_t, patch_weight, patch_bias.reshape(1, channels))

    taps = KSIZE * KSIZE
    taps_w = conv_kernel.reshape(taps, 2, LANES).transpose(1, 0, 2)
    taps_w = jnp.broadcast_to(taps_w[:, :, None, :], (2, taps, 8, LANES))
    gain = norm_gain.reshape(1, channels)
    kv = kv_weight.reshape(channels, 2, HEADS, LANES).transpose(2, 0, 1, 3)
    kv = kv.reshape(HEADS, channels, 2 * LANES)
    kvt = kv.transpose(0, 2, 1)
    q = latents.reshape(count, HEADS, LANES).transpose(1, 0, 2)
    qt = q.transpose(0, 2, 1)
    da = d_attended.reshape(count, HEADS, LANES).transpose(1, 0, 2)
    dat = da.transpose(0, 2, 1)
    params = pltpu.CompilerParams(vmem_limit_bytes=VMEM_LIMIT)
    mixed, proj, stats, weighted = pl.pallas_call(
        functools.partial(forward_kernel, tile_rows, tile_cols),
        grid=(HEADS,),
        in_specs=[
            whole_spec((2, pad_rows, pad_cols, LANES)),
            whole_spec((2, taps, 8, LANES)),
            whole_spec((1, channels)),
            head_spec((channels, 2 * LANES)),
            head_spec((LANES, count)),
            head_spec((LANES, count)),
        ],
        out_specs=[
            whole_spec((2, tile_rows, tile_cols, LANES)),
            head_spec((tokens, 2 * LANES)),
            pl.BlockSpec((3, 1, 1, count), lambda n: (0, n, 0, 0)),
            head_spec((LANES, count)),
        ],
        out_shape=[
            struct(2, tile_rows, tile_cols, LANES),
            struct(HEADS, tokens, 2 * LANES, dtype=bf16),
            struct(3, HEADS, 1, count),
            struct(HEADS, LANES, count),
        ],
        scratch_shapes=[pltpu.VMEM((tokens, channels), bf16), pltpu.VMEM((tokens, count), f32)],
        compiler_params=params,
        name="forward",
    )(x, taps_w, gain, kv, qt, dat)
    shared = mesh_stats(stats.reshape(3, HEADS, count), rows, cols)
    shift, dots = shared.reshape(2, HEADS, 1, count)
    tops = stats[0]
    large, d_mixed, grad_gain = pl.pallas_call(
        functools.partial(backward_kernel, tile_rows, tile_cols),
        grid=(HEADS,),
        in_specs=[
            whole_spec((2, tile_rows, tile_cols, LANES)),
            whole_spec((1, channels)),
            head_spec((tokens, 2 * LANES)),
            head_spec((LANES, count)),
            head_spec((count, LANES)),
            head_spec((LANES, count)),
            head_spec((count, LANES)),
            head_spec((2 * LANES, channels)),
            head_spec((1, count)),
            head_spec((1, count)),
            head_spec((1, count)),
            head_spec((LANES, count)),
        ],
        out_specs=[
            pl.BlockSpec((1, parts, 4 * LANES, LANES), lambda n: (n, 0, 0, 0)),
            whole_spec((2, tile_rows, tile_cols, LANES)),
            whole_spec((1, channels)),
        ],
        out_shape=[
            struct(HEADS, parts, 4 * LANES, LANES, dtype=bf16),
            struct(2, tile_rows, tile_cols, LANES),
            struct(1, channels),
        ],
        scratch_shapes=[
            pltpu.VMEM((tokens, channels), bf16),
            pltpu.VMEM((8, LANES), bf16),
            pltpu.VMEM((tokens, channels), f32),
        ],
        compiler_params=params,
        name="backward",
    )(mixed, gain, proj, qt, q, dat, da, kvt, shift, dots, tops, weighted)
    large, small = closing(large, x, d_mixed, taps_w, patches_t, grad_gain, rows, cols)
    large = large.astype(f32).reshape(HEADS, parts, 4 * LANES, LANES)
    half_rows = small.size // (2 * LANES)
    small = small.reshape(2, half_rows, LANES).transpose(1, 0, 2).reshape(half_rows, channels)
    size = patches_t.shape[0]
    attended = large[:, :, :LANES].transpose(1, 3, 0, 2).reshape(count, model_dim)
    grad_latents = large[:, :, LANES : 2 * LANES].transpose(1, 3, 0, 2).reshape(count, model_dim)
    grad_kv = large[:, :, 2 * LANES :].transpose(2, 1, 0, 3).reshape(channels, 2 * model_dim)
    return (
        attended,
        grad_latents,
        grad_kv,
        small[-1],
        small[size : size + taps],
        small[:size],
        small[-2],
    )


def solution(mesh):
    return jax.shard_map(
        per_device,
        mesh=mesh,
        in_specs=(P(None, "rows", "cols"), P(), P(), P(), P(), P(), P(), P()),
        out_specs=(P(), P(), P(), P(), P(), P(), P()),
        check_vma=False,
    )
```

```python
import functools

import jax
import jax.numpy as jnp
from jax import lax
from jax.experimental import pallas as pl
from jax.experimental.pallas import tpu as pltpu
from jax.sharding import PartitionSpec as P

PATCH = 4
KSIZE = 7
HEADS = 8
HALF = KSIZE // 2
EDGE = 8 - HALF
LANES = 128
GROUP = 8
LOG2E = 1.4426950408889634
VMEM_LIMIT = 56 * 1024 * 1024

norm_eps = 1e-05
f32 = jnp.float32
bf16 = jnp.bfloat16


def patch_columns(pixels):
    fields, height, width = pixels.shape
    place = jnp.arange(width)
    target = (place % PATCH) * (width // PATCH) + place // PATCH
    sort = (target[:, None] == place[None, :]).astype(bf16)
    x = jnp.dot(pixels.reshape(fields * height, width), sort, preferred_element_type=f32)
    x = x.astype(bf16).reshape(fields, height // PATCH, PATCH, PATCH, width // PATCH)
    x = x.transpose(0, 2, 3, 1, 4)
    return x.reshape(fields * PATCH * PATCH, height // PATCH * (width // PATCH))


def conv_windows(x_ref, w_ref, out_ref, tile_rows, tile_cols, flipped, part=None):
    groups = tile_rows // GROUP
    first, last = (0, 2 * groups) if part is None else (part * groups, (part + 1) * groups)

    def body(n, carry):
        h = n // groups
        r0 = (n % groups) * GROUP
        for cb in range(tile_cols // 8):
            acc = x_ref[h, pl.ds(r0 + HALF, GROUP), cb * 8 + 8 : cb * 8 + 16, :].astype(f32)
            for j in range(KSIZE):
                x = x_ref[h, pl.ds(r0, GROUP + KSIZE - 1), cb * 8 + EDGE + j : cb * 8 + EDGE + j + 8, :].astype(f32)
                for i in range(KSIZE):
                    tap = i * KSIZE + j
                    if flipped:
                        tap = KSIZE * KSIZE - 1 - tap
                    acc = acc + x[i : i + GROUP] * w_ref[h, tap][None]
            out_ref[h, pl.ds(r0, GROUP), cb * 8 : cb * 8 + 8, :] = acc
        return carry

    lax.fori_loop(first, last, body, 0)


def norm_rows(m0, m1):
    channels = 2 * LANES
    mean = (jnp.sum(m0, axis=-1, keepdims=True) + jnp.sum(m1, axis=-1, keepdims=True)) / channels
    c0 = m0 - mean
    c1 = m1 - mean
    variance = (
        jnp.sum(c0 * c0, axis=-1, keepdims=True) + jnp.sum(c1 * c1, axis=-1, keepdims=True)
    ) / channels
    inverse = lax.rsqrt(variance + norm_eps)
    return c0 * inverse, c1 * inverse, inverse


def forward_kernel(
    tile_rows, tile_cols, x_ref, w_ref, gain_ref, kv_ref, qt_ref, dat_ref,
    mixed_ref, proj_ref, stats_ref, weighted_ref, normed, scores,
):
    tokens = tile_rows * tile_cols

    @pl.when(pl.program_id(0) == 0)
    def _():
        conv_windows(x_ref, w_ref, mixed_ref, tile_rows, tile_cols, False)

        def body(a, carry):
            c0, c1, _ = norm_rows(mixed_ref[0, a], mixed_ref[1, a])
            rows = pl.ds(pl.multiple_of(a * tile_cols, tile_cols), tile_cols)
            normed[rows, :LANES] = (c0 * gain_ref[:, :LANES]).astype(bf16)
            normed[rows, LANES:] = (c1 * gain_ref[:, LANES:]).astype(bf16)
            return carry

        lax.fori_loop(0, tile_rows, body, 0)

    chunk = 512
    scale = LOG2E * LANES**-0.5
    peak = jnp.full((1, scores.shape[1]), -jnp.inf, f32)
    for n in range(tokens // chunk):
        rows = slice(n * chunk, (n + 1) * chunk)
        proj = jnp.dot(normed[rows, :], kv_ref[0], preferred_element_type=f32).astype(bf16)
        proj_ref[0, rows, :] = proj
        s = jnp.dot(proj[:, :LANES], qt_ref[0], preferred_element_type=f32) * scale
        scores[rows, :] = s
        peak = jnp.maximum(peak, jnp.max(s, axis=0, keepdims=True))
    total = jnp.zeros_like(peak)
    weighted = jnp.zeros((LANES, scores.shape[1]), f32)
    for n in range(tokens // chunk):
        rows = slice(n * chunk, (n + 1) * chunk)
        raised = jnp.exp2(scores[rows, :] - peak)
        total = total + jnp.sum(raised, axis=0, keepdims=True)
        weighted = weighted + lax.dot_general(
            proj_ref[0, rows, LANES:], raised.astype(bf16), (((0,), (0,)), ((), ())),
            preferred_element_type=f32,
        )
    stats_ref[0, 0] = peak
    stats_ref[1, 0] = total
    stats_ref[2, 0] = jnp.sum(weighted * dat_ref[0].astype(f32), axis=0, keepdims=True)
    weighted_ref[0] = weighted


def backward_kernel(
    tile_rows, tile_cols, mixed_ref, gain_ref, proj_ref, qt_ref, q_ref, dat_ref, da_ref,
    kvt_ref, shift_ref, dots_ref, top_ref, weighted_ref,
    large_ref, d_mixed_ref, grad_gain_ref, normed, d_proj, d_normed,
):
    tokens = tile_rows * tile_cols
    chunk = 512
    scale = LANES**-0.5

    @pl.when(pl.program_id(0) == 0)
    def _():
        def body(a, carry):
            c0, c1, _ = norm_rows(mixed_ref[0, a], mixed_ref[1, a])
            rows = pl.ds(pl.multiple_of(a * tile_cols, tile_cols), tile_cols)
            normed[rows, :LANES] = (c0 * gain_ref[:, :LANES]).astype(bf16)
            normed[rows, LANES:] = (c1 * gain_ref[:, LANES:]).astype(bf16)
            d_normed[rows, :] = jnp.zeros((tile_cols, 2 * LANES), f32)
            return carry

        lax.fori_loop(0, tile_rows, body, 0)

    shift = shift_ref[0]
    dots = dots_ref[0]
    grad_q = jnp.zeros((LANES, shift.shape[1]), f32)
    grad_kv = jnp.zeros((2 * LANES, 2 * LANES), f32)
    for n in range(tokens // chunk):
        rows = slice(n * chunk, (n + 1) * chunk)
        keys = proj_ref[0, rows, :LANES]
        values = proj_ref[0, rows, LANES:]
        s = jnp.dot(keys, qt_ref[0], preferred_element_type=f32) * (LOG2E * scale)
        probs = jnp.exp2(s - shift)
        d_probs = jnp.dot(values, dat_ref[0], preferred_element_type=f32)
        d_scores = (probs * (d_probs - dots)).astype(bf16)
        grad_q = grad_q + lax.dot_general(
            keys, d_scores, (((0,), (0,)), ((), ())), preferred_element_type=f32
        )
        d_keys = jnp.dot(d_scores, q_ref[0], preferred_element_type=f32) * scale
        d_values = jnp.dot(probs.astype(bf16), da_ref[0], preferred_element_type=f32)
        both = jnp.concatenate([d_keys.astype(bf16), d_values.astype(bf16)], axis=1)
        d_normed[rows, :] += jnp.dot(both, kvt_ref[0], preferred_element_type=f32)
        grad_kv = grad_kv + lax.dot_general(
            normed[rows, :], both, (((0,), (0,)), ((), ())), preferred_element_type=f32
        )
    attended = weighted_ref[0] * jnp.exp2(top_ref[0] - shift)
    large_ref[0, 0] = attended.T.astype(bf16)
    large_ref[0, 1] = (grad_q * scale).T.astype(bf16)
    large_ref[0, 2] = grad_kv[:, :LANES].astype(bf16)
    large_ref[0, 3] = grad_kv[:, LANES:].astype(bf16)

    @pl.when(pl.program_id(0) == pl.num_programs(0) - 1)
    def _():
        def body(a, carry):
            gg0, gg1 = carry
            c0, c1, inverse = norm_rows(mixed_ref[0, a], mixed_ref[1, a])
            rows = pl.ds(pl.multiple_of(a * tile_cols, tile_cols), tile_cols)
            d0 = d_normed[rows, :LANES]
            d1 = d_normed[rows, LANES:]
            gg0 = gg0 + jnp.sum(d0 * c0, axis=0, keepdims=True)
            gg1 = gg1 + jnp.sum(d1 * c1, axis=0, keepdims=True)
            s0 = d0 * gain_ref[:, :LANES]
            s1 = d1 * gain_ref[:, LANES:]
            mean = (
                jnp.sum(s0, axis=-1, keepdims=True) + jnp.sum(s1, axis=-1, keepdims=True)
            ) / (2 * LANES)
            dot = (
                jnp.sum(s0 * c0, axis=-1, keepdims=True) + jnp.sum(s1 * c1, axis=-1, keepdims=True)
            ) / (2 * LANES)
            m0 = inverse * (s0 - mean - c0 * dot)
            m1 = inverse * (s1 - mean - c1 * dot)
            d_mixed_ref[0, a] = m0.astype(bf16).astype(f32)
            d_mixed_ref[1, a] = m1.astype(bf16).astype(f32)
            return gg0, gg1

        zero = jnp.zeros((1, LANES), f32)
        gg0, gg1 = lax.fori_loop(0, tile_rows, body, (zero, zero))
        grad_gain_ref[:, :LANES] = gg0
        grad_gain_ref[:, LANES:] = gg1


def kernel_grad(x_ref, d_ref, acc_ref, tile_rows, tile_cols, h):
    acc_ref[h] = jnp.zeros(acc_ref.shape[1:], f32)

    def body(n, carry):
        r0 = n * GROUP
        for cb in range(tile_cols // 8):
            d = d_ref[h, pl.ds(r0 + HALF, GROUP), cb * 8 + 8 : cb * 8 + 16, :]
            for j in range(KSIZE):
                lanes = slice(cb * 8 + EDGE + j, cb * 8 + EDGE + j + 8)
                x = x_ref[h, pl.ds(r0, GROUP + KSIZE - 1), lanes, :]
                for i in range(KSIZE):
                    acc_ref[h, i * KSIZE + j] += jnp.sum(x[i : i + GROUP] * d, axis=0)
        return carry

    lax.fori_loop(0, tile_rows // GROUP, body, 0)


MESH = pl.DeviceIdType.MESH


def greet(row, col, rows, cols):
    barrier = pltpu.get_barrier_semaphore()
    for p in range(1, cols):
        pl.semaphore_signal(
            barrier, inc=1, device_id=(row, lax.rem(col + p, cols)), device_id_type=MESH
        )
    for p in range(1, rows):
        pl.semaphore_signal(
            barrier, inc=1, device_id=(lax.rem(row + p, rows), col), device_id_type=MESH
        )
    pl.semaphore_wait(barrier, rows + cols - 2)


def push(src, dst, sems, stage, slot, device):
    copy = pltpu.make_async_remote_copy(
        src_ref=src,
        dst_ref=dst,
        send_sem=sems.at[0, stage, slot],
        recv_sem=sems.at[1, stage, slot],
        device_id=device,
        device_id_type=MESH,
    )
    copy.start()
    return copy


def await_into(dst, sems, stage, slot, device):
    pltpu.make_async_remote_copy(
        src_ref=dst,
        dst_ref=dst,
        send_sem=sems.at[0, stage, slot],
        recv_sem=sems.at[1, stage, slot],
        device_id=device,
        device_id_type=MESH,
    ).wait_recv()


def halo_cols(buf, sems, row, col, cols, tile_rows, tile_cols):
    inner = pl.ds(HALF, tile_rows)

    def part(start):
        return buf.at[:, inner, pl.ds(start, 8), :]

    def copies():
        right = lambda: pltpu.make_async_remote_copy(
            src_ref=part(tile_cols), dst_ref=part(0), send_sem=sems.at[0, 0], recv_sem=sems.at[1, 0],
            device_id=(row, lax.min(col + 1, cols - 1)), device_id_type=MESH,
        )
        left = lambda: pltpu.make_async_remote_copy(
            src_ref=part(8), dst_ref=part(tile_cols + 8), send_sem=sems.at[0, 1], recv_sem=sems.at[1, 1],
            device_id=(row, lax.max(col - 1, 0)), device_id_type=MESH,
        )
        return right, left

    return run_halo(copies, col, cols)


def halo_rows(buf, sems, row, col, rows, tile_rows):
    def part(start):
        return buf.at[:, pl.ds(start, HALF), :, :]

    def copies():
        down = lambda: pltpu.make_async_remote_copy(
            src_ref=part(tile_rows), dst_ref=part(0), send_sem=sems.at[0, 2], recv_sem=sems.at[1, 2],
            device_id=(lax.min(row + 1, rows - 1), col), device_id_type=MESH,
        )
        up = lambda: pltpu.make_async_remote_copy(
            src_ref=part(HALF), dst_ref=part(tile_rows + HALF), send_sem=sems.at[0, 3], recv_sem=sems.at[1, 3],
            device_id=(lax.max(row - 1, 0), col), device_id_type=MESH,
        )
        return down, up

    return run_halo(copies, row, rows)


def run_halo(copies, me, devices):
    @pl.when(me < devices - 1)
    def _():
        copies()[0]().start()

    @pl.when(me > 0)
    def _():
        copies()[1]().start()

    def wait():
        @pl.when(me > 0)
        def _():
            copies()[0]().wait_recv()
            copies()[1]().wait_send()

        @pl.when(me < devices - 1)
        def _():
            copies()[1]().wait_recv()
            copies()[0]().wait_send()

    return wait


class Reduction:
    def __init__(self, x, out, paired, held, first, middle, second, sems):
        self.x, self.out, self.first, self.middle, self.second = x, out, first, middle, second
        self.paired, self.held = paired, held
        self.sems = sems
        self.cols, self.rows = x.shape[:2]
        self.row, self.col = lax.axis_index("rows"), lax.axis_index("cols")
        self.pairs = self.cols // 2
        self.pair, self.side = self.col // 2, lax.rem(self.col, 2)
        self.twin = (self.row, self.pair * 2 + 1 - self.side)
        self.copies = []

    def across(self, p):
        return lax.rem(self.pair + p, self.pairs) * 2 + self.side

    def along(self, p):
        return lax.rem(self.row + p, self.rows)

    def send(self, src, dst, stage, slot, device):
        self.copies.append(push(src, dst, self.sems, stage, slot, device))

    def send_pair(self):
        for k in range(self.pairs):
            self.send(self.x.at[2 * k + 1 - self.side], self.paired.at[k], 0, k, self.twin)

    def sum_pair(self):
        for k in range(self.pairs):
            await_into(self.paired.at[k], self.sems, 0, k, self.twin)

        def body(n, carry):
            k, r = n // self.rows, n % self.rows
            acc = self.x[2 * k + self.side, r].astype(f32) + self.paired[k, r].astype(f32)
            self.held[k, r] = acc.astype(self.held.dtype)
            return carry

        lax.fori_loop(0, self.pairs * self.rows, body, 0)
        for p in range(1, self.pairs):
            there = lax.rem(self.pair + p, self.pairs)
            self.send(self.held.at[there], self.first.at[p], 1, p, (self.row, self.across(p)))

    def sum_cols(self):
        for p in range(1, self.pairs):
            source = (self.row, self.across(self.pairs - p))
            await_into(self.first.at[p], self.sems, 1, p, source)

        def body(r, carry):
            acc = self.held[self.pair, r].astype(f32)
            for p in range(1, self.pairs):
                acc = acc + self.first[p, r].astype(f32)
            self.middle[r] = acc.astype(self.middle.dtype)
            return carry

        lax.fori_loop(0, self.rows, body, 0)
        for p in range(1, self.rows):
            there = self.along(p)
            self.send(self.middle.at[there], self.second.at[p], 2, p, (there, self.col))

    def sum_rows(self):
        for p in range(1, self.rows):
            source = (self.along(self.rows - p), self.col)
            await_into(self.second.at[p], self.sems, 2, p, source)
        acc = self.middle[self.row].astype(f32)
        for p in range(1, self.rows):
            acc = acc + self.second[p].astype(f32)
        self.out[self.col, self.row] = acc.astype(self.out.dtype)
        piece = self.out.at[self.col, self.row]
        for p in range(1, self.rows):
            self.send(piece, piece, 3, p, (self.along(p), self.col))

    def spread_cols(self):
        for p in range(1, self.rows):
            source = self.along(self.rows - p)
            await_into(self.out.at[self.col, source], self.sems, 3, p, (source, self.col))
        slab = self.out.at[self.col]
        for p in range(1, self.pairs):
            self.send(slab, slab, 4, p, (self.row, self.across(p)))
        self.send(slab, slab, 5, 0, self.twin)

    def spread_pair(self):
        for p in range(1, self.pairs):
            source = self.across(self.pairs - p)
            slab = self.out.at[source]
            await_into(slab, self.sems, 4, p, (self.row, source))
            self.send(slab, slab, 5, p, self.twin)
        for p in range(self.pairs):
            source = lax.rem(self.pair + self.pairs - p, self.pairs) * 2 + 1 - self.side
            await_into(self.out.at[source], self.sems, 5, p, self.twin)
        for copy in self.copies:
            copy.wait_send()


def embed_kernel(rows, cols, tile_rows, tile_cols, patches_ref, w_ref, bias_ref, out_ref, buf, sems):
    row, col = lax.axis_index("rows"), lax.axis_index("cols")
    embedded = lax.dot_general(
        patches_ref[...], w_ref[...], (((0,), (0,)), ((), ())), preferred_element_type=f32
    )
    embedded = (embedded + bias_ref[...]).astype(bf16).astype(f32)
    buf[...] = jnp.zeros_like(buf)
    for h in range(2):
        tile = embedded[:, h * LANES : (h + 1) * LANES].reshape(tile_rows, tile_cols, LANES)
        buf[h, HALF : HALF + tile_rows, 8 : 8 + tile_cols, :] = tile
    greet(row, col, rows, cols)
    halo_cols(buf, sems, row, col, cols, tile_rows, tile_cols)()
    halo_rows(buf, sems, row, col, rows, tile_rows)()
    out_ref[...] = buf[...]


def closing_kernel(
    tile_rows, tile_cols, large_ref, x_ref, d_ref, w_ref, patches_ref, gain_ref,
    large_out, small_out,
    buf, acc, out, flat, small, paired, held, first, middle, second,
    s_paired, s_held, s_first, s_middle, s_second,
    halo_sems, sems, s_sems,
):
    cols, rows = large_ref.shape[:2]
    row, col = lax.axis_index("rows"), lax.axis_index("cols")
    taps = KSIZE * KSIZE
    buf[...] = jnp.zeros_like(buf)
    buf[:, HALF : HALF + tile_rows, 8 : 8 + tile_cols, :] = d_ref[...]
    flat[...] = jnp.zeros_like(flat)
    greet(row, col, rows, cols)
    big = Reduction(large_ref, large_out, paired, held, first, middle, second, sems)
    little = Reduction(small, small_out, s_paired, s_held, s_first, s_middle, s_second, s_sems)
    wait = halo_cols(buf, halo_sems, row, col, cols, tile_rows, tile_cols)
    big.send_pair()
    kernel_grad(x_ref, d_ref=buf, acc_ref=acc, tile_rows=tile_rows, tile_cols=tile_cols, h=0)
    big.sum_pair()
    wait()
    wait = halo_rows(buf, halo_sems, row, col, rows, tile_rows)
    kernel_grad(x_ref, d_ref=buf, acc_ref=acc, tile_rows=tile_rows, tile_cols=tile_cols, h=1)
    wait()
    patch_size = patches_ref.shape[0]
    part = flat.shape[0] // 2
    for h in range(2):
        conv_windows(buf, w_ref, out, tile_rows, tile_cols, True, h)
        d = out[h].reshape(tile_rows * tile_cols, LANES).astype(bf16)
        base = h * part
        flat[base : base + patch_size, :] = jnp.dot(
            patches_ref[...], d, preferred_element_type=f32
        )
        flat[base + patch_size : base + patch_size + taps, :] = jnp.sum(acc[h], axis=1)
        flat[base + part - 2 : base + part - 1, :] = jnp.sum(d.astype(f32), axis=0, keepdims=True)
        flat[base + part - 1 : base + part, :] = gain_ref[:, h * LANES : (h + 1) * LANES]
        if h == 0:
            big.sum_cols()
    for n in range(cols * rows):
        block = small.shape[2]
        small[n // rows, n % rows] = flat[n * block : (n + 1) * block, :]
    little.send_pair()
    big.sum_rows()
    little.sum_pair()
    big.spread_cols()
    little.sum_cols()
    little.sum_rows()
    little.spread_cols()
    little.spread_pair()
    big.spread_pair()


def closing(large, x, d_mixed, taps_w, patches_t, grad_gain, rows, cols):
    _, tile_rows, tile_cols, _ = d_mixed.shape
    n = large.size // (rows * cols * LANES)
    large = large.reshape(cols, rows, n, LANES)
    pieces = rows * cols
    needed = 2 * (patches_t.shape[0] + KSIZE * KSIZE + 2)
    m = pl.cdiv(needed, pieces * 8) * 8
    vmem = pl.BlockSpec(memory_space=pltpu.VMEM)
    return pl.pallas_call(
        functools.partial(closing_kernel, tile_rows, tile_cols),
        out_shape=[struct(cols, rows, n, LANES, dtype=bf16), struct(cols, rows, m, LANES)],
        in_specs=[vmem] * 6,
        out_specs=[vmem] * 2,
        scratch_shapes=[
            pltpu.VMEM((2, tile_rows + 2 * HALF, tile_cols + 16, LANES), f32),
            pltpu.VMEM((2, KSIZE * KSIZE, 8, LANES), f32),
            pltpu.VMEM((2, tile_rows, tile_cols, LANES), f32),
            pltpu.VMEM((pieces * m, LANES), f32),
            pltpu.VMEM((cols, rows, m, LANES), f32),
            pltpu.VMEM((cols // 2, rows, n, LANES), bf16),
            pltpu.VMEM((cols // 2, rows, n, LANES), bf16),
            pltpu.VMEM((cols // 2, rows, n, LANES), bf16),
            pltpu.VMEM((rows, n, LANES), bf16),
            pltpu.VMEM((rows, n, LANES), bf16),
            pltpu.VMEM((cols // 2, rows, m, LANES), f32),
            pltpu.VMEM((cols // 2, rows, m, LANES), f32),
            pltpu.VMEM((cols // 2, rows, m, LANES), f32),
            pltpu.VMEM((rows, m, LANES), f32),
            pltpu.VMEM((rows, m, LANES), f32),
            pltpu.SemaphoreType.DMA((2, 4)),
            pltpu.SemaphoreType.DMA((2, 6, max(rows, cols))),
            pltpu.SemaphoreType.DMA((2, 6, max(rows, cols))),
        ],
        compiler_params=pltpu.CompilerParams(
            collective_id=2, has_side_effects=True, vmem_limit_bytes=VMEM_LIMIT
        ),
        name="closing",
    )(large, x, d_mixed, taps_w, patches_t, grad_gain)


def combine(stats):
    peak = jnp.max(stats[:, 0], axis=0)
    factor = jnp.exp2(stats[:, 0] - peak[None])
    return jnp.stack(
        [peak, jnp.sum(stats[:, 1] * factor, axis=0), jnp.sum(stats[:, 2] * factor, axis=0)]
    )


def stats_kernel(rows, cols, x_ref, out_ref, first, second, sems):
    row, col = lax.axis_index("rows"), lax.axis_index("cols")
    greet(row, col, rows, cols)
    copies = []
    first[0] = x_ref[...]
    for p in range(1, cols):
        there = (row, lax.rem(col + p, cols))
        copies.append(push(x_ref, first.at[p], sems, 0, p, there))
    for p in range(1, cols):
        await_into(first.at[p], sems, 0, p, (row, lax.rem(col + cols - p, cols)))
    second[0] = combine(first[...])
    for p in range(1, rows):
        there = (lax.rem(row + p, rows), col)
        copies.append(push(second.at[0], second.at[p], sems, 1, p, there))
    for p in range(1, rows):
        await_into(second.at[p], sems, 1, p, (lax.rem(row + rows - p, rows), col))
    total = combine(second[...])
    out_ref[0] = total[0] + jnp.log2(total[1])
    out_ref[1] = total[2] / total[1]
    for copy in copies:
        copy.wait_send()


def mesh_stats(x, rows, cols):
    vmem = pl.BlockSpec(memory_space=pltpu.VMEM)
    return pl.pallas_call(
        functools.partial(stats_kernel, rows, cols),
        out_shape=struct(2, *x.shape[1:]),
        in_specs=[vmem],
        out_specs=vmem,
        scratch_shapes=[
            pltpu.VMEM((cols,) + x.shape, f32),
            pltpu.VMEM((rows,) + x.shape, f32),
            pltpu.SemaphoreType.DMA((2, 2, max(rows, cols))),
        ],
        compiler_params=pltpu.CompilerParams(
            collective_id=1, has_side_effects=True, vmem_limit_bytes=VMEM_LIMIT
        ),
        name="stats",
    )(x)


def format_kernel(large_ref, attended_ref, grad_q_ref, grad_kv_ref):
    attended_ref[...] = large_ref[0, 0].astype(f32)
    grad_q_ref[...] = large_ref[0, 1].astype(f32)
    head = pl.program_id(0)
    width = grad_kv_ref.shape[1] // 2
    keys = pl.ds(pl.multiple_of(head * LANES, LANES), LANES)
    values = pl.ds(pl.multiple_of(width + head * LANES, LANES), LANES)
    grad_kv_ref[:, keys] = large_ref[0, 2].astype(f32)
    grad_kv_ref[:, values] = large_ref[0, 3].astype(f32)


def head_spec(shape):
    return pl.BlockSpec((1,) + shape, lambda n: (n, 0, 0))


def whole_spec(shape):
    return pl.BlockSpec(shape, lambda n: (0,) * len(shape))


def struct(*shape, dtype=f32):
    return jax.ShapeDtypeStruct(shape, dtype)


def per_device(
    pixels, patch_weight, patch_bias, conv_kernel, norm_gain, kv_weight, latents, d_attended
):
    tile_rows = pixels.shape[1] // PATCH
    tile_cols = pixels.shape[2] // PATCH
    tokens = tile_rows * tile_cols
    channels = patch_weight.shape[1]
    count, model_dim = latents.shape
    parts = count // LANES
    rows, cols = lax.axis_size("rows"), lax.axis_size("cols")
    patches_t = patch_columns(pixels)
    pad_rows, pad_cols = tile_rows + 2 * HALF, tile_cols + 16
    vmem = pl.BlockSpec(memory_space=pltpu.VMEM)
    x = pl.pallas_call(
        functools.partial(embed_kernel, rows, cols, tile_rows, tile_cols),
        out_shape=struct(2, pad_rows, pad_cols, LANES),
        in_specs=[vmem] * 3,
        out_specs=vmem,
        scratch_shapes=[
            pltpu.VMEM((2, pad_rows, pad_cols, LANES), f32),
            pltpu.SemaphoreType.DMA((2, 4)),
        ],
        compiler_params=pltpu.CompilerParams(
            collective_id=3, has_side_effects=True, vmem_limit_bytes=VMEM_LIMIT
        ),
        name="embed",
    )(patches_t, patch_weight, patch_bias.reshape(1, channels))

    taps = KSIZE * KSIZE
    taps_w = conv_kernel.reshape(taps, 2, LANES).transpose(1, 0, 2)
    taps_w = jnp.broadcast_to(taps_w[:, :, None, :], (2, taps, 8, LANES))
    gain = norm_gain.reshape(1, channels)
    kv = kv_weight.reshape(channels, 2, HEADS, LANES).transpose(2, 0, 1, 3)
    kv = kv.reshape(HEADS, channels, 2 * LANES)
    kvt = kv.transpose(0, 2, 1)
    q = latents.reshape(count, HEADS, LANES).transpose(1, 0, 2)
    qt = q.transpose(0, 2, 1)
    da = d_attended.reshape(count, HEADS, LANES).transpose(1, 0, 2)
    dat = da.transpose(0, 2, 1)
    params = pltpu.CompilerParams(vmem_limit_bytes=VMEM_LIMIT)
    mixed, proj, stats, weighted = pl.pallas_call(
        functools.partial(forward_kernel, tile_rows, tile_cols),
        grid=(HEADS,),
        in_specs=[
            whole_spec((2, pad_rows, pad_cols, LANES)),
            whole_spec((2, taps, 8, LANES)),
            whole_spec((1, channels)),
            head_spec((channels, 2 * LANES)),
            head_spec((LANES, count)),
            head_spec((LANES, count)),
        ],
        out_specs=[
            whole_spec((2, tile_rows, tile_cols, LANES)),
            head_spec((tokens, 2 * LANES)),
            pl.BlockSpec((3, 1, 1, count), lambda n: (0, n, 0, 0)),
            head_spec((LANES, count)),
        ],
        out_shape=[
            struct(2, tile_rows, tile_cols, LANES),
            struct(HEADS, tokens, 2 * LANES, dtype=bf16),
            struct(3, HEADS, 1, count),
            struct(HEADS, LANES, count),
        ],
        scratch_shapes=[pltpu.VMEM((tokens, channels), bf16), pltpu.VMEM((tokens, count), f32)],
        compiler_params=params,
        name="forward",
    )(x, taps_w, gain, kv, qt, dat)
    shared = mesh_stats(stats.reshape(3, HEADS, count), rows, cols)
    shift, dots = shared.reshape(2, HEADS, 1, count)
    tops = stats[0]
    large, d_mixed, grad_gain = pl.pallas_call(
        functools.partial(backward_kernel, tile_rows, tile_cols),
        grid=(HEADS,),
        in_specs=[
            whole_spec((2, tile_rows, tile_cols, LANES)),
            whole_spec((1, channels)),
            head_spec((tokens, 2 * LANES)),
            head_spec((LANES, count)),
            head_spec((count, LANES)),
            head_spec((LANES, count)),
            head_spec((count, LANES)),
            head_spec((2 * LANES, channels)),
            head_spec((1, count)),
            head_spec((1, count)),
            head_spec((1, count)),
            head_spec((LANES, count)),
        ],
        out_specs=[
            pl.BlockSpec((1, 4, channels, LANES), lambda n: (n, 0, 0, 0)),
            whole_spec((2, tile_rows, tile_cols, LANES)),
            whole_spec((1, channels)),
        ],
        out_shape=[
            struct(HEADS, 4, channels, LANES, dtype=bf16),
            struct(2, tile_rows, tile_cols, LANES),
            struct(1, channels),
        ],
        scratch_shapes=[
            pltpu.VMEM((tokens, channels), bf16),
            pltpu.VMEM((8, LANES), bf16),
            pltpu.VMEM((tokens, channels), f32),
        ],
        compiler_params=params,
        name="backward",
    )(mixed, gain, proj, qt, q, dat, da, kvt, shift, dots, tops, weighted)
    large, small = closing(large, x, d_mixed, taps_w, patches_t, grad_gain, rows, cols)
    attended, grad_latents, grad_kv = pl.pallas_call(
        format_kernel,
        grid=(HEADS,),
        in_specs=[pl.BlockSpec((1, 4, count, LANES), lambda n: (n, 0, 0, 0))],
        out_specs=[
            pl.BlockSpec((count, LANES), lambda n: (0, n)),
            pl.BlockSpec((count, LANES), lambda n: (0, n)),
            whole_spec((channels, 2 * model_dim)),
        ],
        out_shape=[
            struct(count, model_dim), struct(count, model_dim), struct(channels, 2 * model_dim)
        ],
        name="outputs",
    )(large.reshape(HEADS, 4, count, LANES))
    half_rows = small.size // (2 * LANES)
    small = small.reshape(2, half_rows, LANES).transpose(1, 0, 2).reshape(half_rows, channels)
    size = patches_t.shape[0]
    return (
        attended,
        grad_latents,
        grad_kv,
        small[-1],
        small[size : size + taps],
        small[:size],
        small[-2],
    )


def solution(mesh):
    return jax.shard_map(
        per_device,
        mesh=mesh,
        in_specs=(P(None, "rows", "cols"), P(), P(), P(), P(), P(), P(), P()),
        out_specs=(P(), P(), P(), P(), P(), P(), P()),
        check_vma=False,
    )
```

```python
import functools

import jax
import jax.numpy as jnp
from jax import lax
from jax.experimental import pallas as pl
from jax.experimental.pallas import tpu as pltpu
from jax.sharding import PartitionSpec as P

PATCH = 4
KSIZE = 7
HEADS = 8
HALF = KSIZE // 2
EDGE = 8 - HALF
LANES = 128
GROUP = 8
LOG2E = 1.4426950408889634
VMEM_LIMIT = 56 * 1024 * 1024

norm_eps = 1e-05
f32 = jnp.float32
bf16 = jnp.bfloat16


def patch_columns(pixels):
    fields, height, width = pixels.shape
    place = jnp.arange(width)
    target = (place % PATCH) * (width // PATCH) + place // PATCH
    sort = (target[:, None] == place[None, :]).astype(bf16)
    x = jnp.dot(pixels.reshape(fields * height, width), sort, preferred_element_type=f32)
    x = x.astype(bf16).reshape(fields, height // PATCH, PATCH, PATCH, width // PATCH)
    x = x.transpose(0, 2, 3, 1, 4)
    return x.reshape(fields * PATCH * PATCH, height // PATCH * (width // PATCH))


def conv_windows(x_ref, w_ref, out_ref, tile_rows, tile_cols, flipped, part=None):
    groups = tile_rows // GROUP
    first, last = (0, 2 * groups) if part is None else (part * groups, (part + 1) * groups)

    def body(n, carry):
        h = n // groups
        r0 = (n % groups) * GROUP
        for cb in range(tile_cols // 8):
            acc = x_ref[h, pl.ds(r0 + HALF, GROUP), cb * 8 + 8 : cb * 8 + 16, :].astype(f32)
            for j in range(KSIZE):
                x = x_ref[h, pl.ds(r0, GROUP + KSIZE - 1), cb * 8 + EDGE + j : cb * 8 + EDGE + j + 8, :].astype(f32)
                for i in range(KSIZE):
                    tap = i * KSIZE + j
                    if flipped:
                        tap = KSIZE * KSIZE - 1 - tap
                    acc = acc + x[i : i + GROUP] * w_ref[h, tap][None]
            out_ref[h, pl.ds(r0, GROUP), cb * 8 : cb * 8 + 8, :] = acc
        return carry

    lax.fori_loop(first, last, body, 0)


def norm_rows(m0, m1):
    channels = 2 * LANES
    mean = (jnp.sum(m0, axis=-1, keepdims=True) + jnp.sum(m1, axis=-1, keepdims=True)) / channels
    c0 = m0 - mean
    c1 = m1 - mean
    variance = (
        jnp.sum(c0 * c0, axis=-1, keepdims=True) + jnp.sum(c1 * c1, axis=-1, keepdims=True)
    ) / channels
    inverse = lax.rsqrt(variance + norm_eps)
    return c0 * inverse, c1 * inverse, inverse


def forward_kernel(
    tile_rows, tile_cols, x_ref, w_ref, gain_ref, kv_ref, qt_ref, dat_ref,
    mixed_ref, proj_ref, stats_ref, weighted_ref, normed, scores,
):
    tokens = tile_rows * tile_cols

    @pl.when(pl.program_id(0) == 0)
    def _():
        conv_windows(x_ref, w_ref, mixed_ref, tile_rows, tile_cols, False)

        def body(a, carry):
            c0, c1, _ = norm_rows(mixed_ref[0, a], mixed_ref[1, a])
            rows = pl.ds(pl.multiple_of(a * tile_cols, tile_cols), tile_cols)
            normed[rows, :LANES] = (c0 * gain_ref[:, :LANES]).astype(bf16)
            normed[rows, LANES:] = (c1 * gain_ref[:, LANES:]).astype(bf16)
            return carry

        lax.fori_loop(0, tile_rows, body, 0)

    chunk = 512
    scale = LOG2E * LANES**-0.5
    peak = jnp.full((1, scores.shape[1]), -jnp.inf, f32)
    for n in range(tokens // chunk):
        rows = slice(n * chunk, (n + 1) * chunk)
        proj = jnp.dot(normed[rows, :], kv_ref[0], preferred_element_type=f32).astype(bf16)
        proj_ref[0, rows, :] = proj
        s = jnp.dot(proj[:, :LANES], qt_ref[0], preferred_element_type=f32) * scale
        scores[rows, :] = s
        peak = jnp.maximum(peak, jnp.max(s, axis=0, keepdims=True))
    total = jnp.zeros_like(peak)
    weighted = jnp.zeros((LANES, scores.shape[1]), f32)
    for n in range(tokens // chunk):
        rows = slice(n * chunk, (n + 1) * chunk)
        raised = jnp.exp2(scores[rows, :] - peak)
        total = total + jnp.sum(raised, axis=0, keepdims=True)
        weighted = weighted + lax.dot_general(
            proj_ref[0, rows, LANES:], raised.astype(bf16), (((0,), (0,)), ((), ())),
            preferred_element_type=f32,
        )
    stats_ref[0, 0] = peak
    stats_ref[1, 0] = total
    stats_ref[2, 0] = jnp.sum(weighted * dat_ref[0].astype(f32), axis=0, keepdims=True)
    weighted_ref[0] = weighted


def backward_kernel(
    tile_rows, tile_cols, mixed_ref, gain_ref, proj_ref, qt_ref, q_ref, dat_ref, da_ref,
    kvt_ref, shared_ref, stats_ref, weighted_ref,
    large_ref, d_mixed_ref, grad_gain_ref, normed, d_proj, d_normed,
):
    tokens = tile_rows * tile_cols
    chunk = 512
    scale = LANES**-0.5

    @pl.when(pl.program_id(0) == 0)
    def _():
        def body(a, carry):
            c0, c1, _ = norm_rows(mixed_ref[0, a], mixed_ref[1, a])
            rows = pl.ds(pl.multiple_of(a * tile_cols, tile_cols), tile_cols)
            normed[rows, :LANES] = (c0 * gain_ref[:, :LANES]).astype(bf16)
            normed[rows, LANES:] = (c1 * gain_ref[:, LANES:]).astype(bf16)
            d_normed[rows, :] = jnp.zeros((tile_cols, 2 * LANES), f32)
            return carry

        lax.fori_loop(0, tile_rows, body, 0)

    shift = shared_ref[0, 0]
    dots = shared_ref[1, 0]
    grad_q = jnp.zeros((LANES, shift.shape[1]), f32)
    grad_kv = jnp.zeros((2 * LANES, 2 * LANES), f32)
    for n in range(tokens // chunk):
        rows = slice(n * chunk, (n + 1) * chunk)
        keys = proj_ref[0, rows, :LANES]
        values = proj_ref[0, rows, LANES:]
        s = jnp.dot(keys, qt_ref[0], preferred_element_type=f32) * (LOG2E * scale)
        probs = jnp.exp2(s - shift)
        d_probs = jnp.dot(values, dat_ref[0], preferred_element_type=f32)
        d_scores = (probs * (d_probs - dots)).astype(bf16)
        grad_q = grad_q + lax.dot_general(
            keys, d_scores, (((0,), (0,)), ((), ())), preferred_element_type=f32
        )
        d_keys = jnp.dot(d_scores, q_ref[0], preferred_element_type=f32) * scale
        d_values = jnp.dot(probs.astype(bf16), da_ref[0], preferred_element_type=f32)
        both = jnp.concatenate([d_keys.astype(bf16), d_values.astype(bf16)], axis=1)
        d_normed[rows, :] += jnp.dot(both, kvt_ref[0], preferred_element_type=f32)
        grad_kv = grad_kv + lax.dot_general(
            normed[rows, :], both, (((0,), (0,)), ((), ())), preferred_element_type=f32
        )
    attended = weighted_ref[0] * jnp.exp2(stats_ref[0, 0] - shift)
    large_ref[0, 0] = attended.T.astype(bf16)
    large_ref[0, 1] = (grad_q * scale).T.astype(bf16)
    large_ref[0, 2] = grad_kv[:, :LANES].astype(bf16)
    large_ref[0, 3] = grad_kv[:, LANES:].astype(bf16)

    @pl.when(pl.program_id(0) == pl.num_programs(0) - 1)
    def _():
        def body(a, carry):
            gg0, gg1 = carry
            c0, c1, inverse = norm_rows(mixed_ref[0, a], mixed_ref[1, a])
            rows = pl.ds(pl.multiple_of(a * tile_cols, tile_cols), tile_cols)
            d0 = d_normed[rows, :LANES]
            d1 = d_normed[rows, LANES:]
            gg0 = gg0 + jnp.sum(d0 * c0, axis=0, keepdims=True)
            gg1 = gg1 + jnp.sum(d1 * c1, axis=0, keepdims=True)
            s0 = d0 * gain_ref[:, :LANES]
            s1 = d1 * gain_ref[:, LANES:]
            mean = (
                jnp.sum(s0, axis=-1, keepdims=True) + jnp.sum(s1, axis=-1, keepdims=True)
            ) / (2 * LANES)
            dot = (
                jnp.sum(s0 * c0, axis=-1, keepdims=True) + jnp.sum(s1 * c1, axis=-1, keepdims=True)
            ) / (2 * LANES)
            m0 = inverse * (s0 - mean - c0 * dot)
            m1 = inverse * (s1 - mean - c1 * dot)
            d_mixed_ref[0, a] = m0.astype(bf16).astype(f32)
            d_mixed_ref[1, a] = m1.astype(bf16).astype(f32)
            return gg0, gg1

        zero = jnp.zeros((1, LANES), f32)
        gg0, gg1 = lax.fori_loop(0, tile_rows, body, (zero, zero))
        grad_gain_ref[:, :LANES] = gg0
        grad_gain_ref[:, LANES:] = gg1


def kernel_grad(x_ref, d_ref, acc_ref, tile_rows, tile_cols, h):
    acc_ref[h] = jnp.zeros(acc_ref.shape[1:], f32)

    def body(n, carry):
        r0 = n * GROUP
        for cb in range(tile_cols // 8):
            d = d_ref[h, pl.ds(r0 + HALF, GROUP), cb * 8 + 8 : cb * 8 + 16, :]
            for j in range(KSIZE):
                lanes = slice(cb * 8 + EDGE + j, cb * 8 + EDGE + j + 8)
                x = x_ref[h, pl.ds(r0, GROUP + KSIZE - 1), lanes, :]
                for i in range(KSIZE):
                    acc_ref[h, i * KSIZE + j] += jnp.sum(x[i : i + GROUP] * d, axis=0)
        return carry

    lax.fori_loop(0, tile_rows // GROUP, body, 0)


MESH = pl.DeviceIdType.MESH


def greet(row, col, rows, cols):
    barrier = pltpu.get_barrier_semaphore()
    for p in range(1, cols):
        pl.semaphore_signal(
            barrier, inc=1, device_id=(row, lax.rem(col + p, cols)), device_id_type=MESH
        )
    for p in range(1, rows):
        pl.semaphore_signal(
            barrier, inc=1, device_id=(lax.rem(row + p, rows), col), device_id_type=MESH
        )
    pl.semaphore_wait(barrier, rows + cols - 2)


def push(src, dst, sems, stage, slot, device):
    copy = pltpu.make_async_remote_copy(
        src_ref=src,
        dst_ref=dst,
        send_sem=sems.at[0, stage, slot],
        recv_sem=sems.at[1, stage, slot],
        device_id=device,
        device_id_type=MESH,
    )
    copy.start()
    return copy


def await_into(dst, sems, stage, slot, device):
    pltpu.make_async_remote_copy(
        src_ref=dst,
        dst_ref=dst,
        send_sem=sems.at[0, stage, slot],
        recv_sem=sems.at[1, stage, slot],
        device_id=device,
        device_id_type=MESH,
    ).wait_recv()


def halo_cols(buf, sems, row, col, cols, tile_rows, tile_cols):
    inner = pl.ds(HALF, tile_rows)

    def part(start):
        return buf.at[:, inner, pl.ds(start, 8), :]

    def copies():
        right = lambda: pltpu.make_async_remote_copy(
            src_ref=part(tile_cols), dst_ref=part(0), send_sem=sems.at[0, 0], recv_sem=sems.at[1, 0],
            device_id=(row, lax.min(col + 1, cols - 1)), device_id_type=MESH,
        )
        left = lambda: pltpu.make_async_remote_copy(
            src_ref=part(8), dst_ref=part(tile_cols + 8), send_sem=sems.at[0, 1], recv_sem=sems.at[1, 1],
            device_id=(row, lax.max(col - 1, 0)), device_id_type=MESH,
        )
        return right, left

    return run_halo(copies, col, cols)


def halo_rows(buf, sems, row, col, rows, tile_rows):
    def part(start):
        return buf.at[:, pl.ds(start, HALF), :, :]

    def copies():
        down = lambda: pltpu.make_async_remote_copy(
            src_ref=part(tile_rows), dst_ref=part(0), send_sem=sems.at[0, 2], recv_sem=sems.at[1, 2],
            device_id=(lax.min(row + 1, rows - 1), col), device_id_type=MESH,
        )
        up = lambda: pltpu.make_async_remote_copy(
            src_ref=part(HALF), dst_ref=part(tile_rows + HALF), send_sem=sems.at[0, 3], recv_sem=sems.at[1, 3],
            device_id=(lax.max(row - 1, 0), col), device_id_type=MESH,
        )
        return down, up

    return run_halo(copies, row, rows)


def run_halo(copies, me, devices):
    @pl.when(me < devices - 1)
    def _():
        copies()[0]().start()

    @pl.when(me > 0)
    def _():
        copies()[1]().start()

    def wait():
        @pl.when(me > 0)
        def _():
            copies()[0]().wait_recv()
            copies()[1]().wait_send()

        @pl.when(me < devices - 1)
        def _():
            copies()[1]().wait_recv()
            copies()[0]().wait_send()

    return wait


class Reduction:
    def __init__(self, x, out, paired, held, first, middle, second, sems):
        self.x, self.out, self.first, self.middle, self.second = x, out, first, middle, second
        self.paired, self.held = paired, held
        self.sems = sems
        self.cols, self.rows = x.shape[:2]
        self.row, self.col = lax.axis_index("rows"), lax.axis_index("cols")
        self.pairs = self.cols // 2
        self.pair, self.side = self.col // 2, lax.rem(self.col, 2)
        self.twin = (self.row, self.pair * 2 + 1 - self.side)
        self.copies = []

    def across(self, p):
        return lax.rem(self.pair + p, self.pairs) * 2 + self.side

    def along(self, p):
        return lax.rem(self.row + p, self.rows)

    def send(self, src, dst, stage, slot, device):
        self.copies.append(push(src, dst, self.sems, stage, slot, device))

    def send_pair(self):
        for k in range(self.pairs):
            self.send(self.x.at[2 * k + 1 - self.side], self.paired.at[k], 0, k, self.twin)

    def sum_pair(self):
        for k in range(self.pairs):
            await_into(self.paired.at[k], self.sems, 0, k, self.twin)

        def body(n, carry):
            k, r = n // self.rows, n % self.rows
            acc = self.x[2 * k + self.side, r].astype(f32) + self.paired[k, r].astype(f32)
            self.held[k, r] = acc.astype(self.held.dtype)
            return carry

        lax.fori_loop(0, self.pairs * self.rows, body, 0)
        for p in range(1, self.pairs):
            there = lax.rem(self.pair + p, self.pairs)
            self.send(self.held.at[there], self.first.at[p], 1, p, (self.row, self.across(p)))

    def sum_cols(self):
        for p in range(1, self.pairs):
            source = (self.row, self.across(self.pairs - p))
            await_into(self.first.at[p], self.sems, 1, p, source)

        def body(r, carry):
            acc = self.held[self.pair, r].astype(f32)
            for p in range(1, self.pairs):
                acc = acc + self.first[p, r].astype(f32)
            self.middle[r] = acc.astype(self.middle.dtype)
            return carry

        lax.fori_loop(0, self.rows, body, 0)
        for p in range(1, self.rows):
            there = self.along(p)
            self.send(self.middle.at[there], self.second.at[p], 2, p, (there, self.col))

    def sum_rows(self):
        for p in range(1, self.rows):
            source = (self.along(self.rows - p), self.col)
            await_into(self.second.at[p], self.sems, 2, p, source)
        acc = self.middle[self.row].astype(f32)
        for p in range(1, self.rows):
            acc = acc + self.second[p].astype(f32)
        self.out[self.col, self.row] = acc.astype(self.out.dtype)
        piece = self.out.at[self.col, self.row]
        for p in range(1, self.rows):
            self.send(piece, piece, 3, p, (self.along(p), self.col))

    def spread_cols(self):
        for p in range(1, self.rows):
            source = self.along(self.rows - p)
            await_into(self.out.at[self.col, source], self.sems, 3, p, (source, self.col))
        slab = self.out.at[self.col]
        for p in range(1, self.pairs):
            self.send(slab, slab, 4, p, (self.row, self.across(p)))
        self.send(slab, slab, 5, 0, self.twin)

    def spread_pair(self):
        for p in range(1, self.pairs):
            source = self.across(self.pairs - p)
            slab = self.out.at[source]
            await_into(slab, self.sems, 4, p, (self.row, source))
            self.send(slab, slab, 5, p, self.twin)
        for p in range(self.pairs):
            source = lax.rem(self.pair + self.pairs - p, self.pairs) * 2 + 1 - self.side
            await_into(self.out.at[source], self.sems, 5, p, self.twin)
        for copy in self.copies:
            copy.wait_send()


def embed_kernel(rows, cols, tile_rows, tile_cols, patches_ref, w_ref, bias_ref, out_ref, buf, sems):
    row, col = lax.axis_index("rows"), lax.axis_index("cols")
    embedded = lax.dot_general(
        patches_ref[...], w_ref[...], (((0,), (0,)), ((), ())), preferred_element_type=f32
    )
    embedded = (embedded + bias_ref[...]).astype(bf16).astype(f32)
    buf[...] = jnp.zeros_like(buf)
    for h in range(2):
        tile = embedded[:, h * LANES : (h + 1) * LANES].reshape(tile_rows, tile_cols, LANES)
        buf[h, HALF : HALF + tile_rows, 8 : 8 + tile_cols, :] = tile
    greet(row, col, rows, cols)
    halo_cols(buf, sems, row, col, cols, tile_rows, tile_cols)()
    halo_rows(buf, sems, row, col, rows, tile_rows)()
    out_ref[...] = buf[...]


def closing_kernel(
    tile_rows, tile_cols, large_ref, x_ref, d_ref, w_ref, patches_ref, gain_ref,
    large_out, small_out,
    buf, acc, out, flat, small, paired, held, first, middle, second,
    s_paired, s_held, s_first, s_middle, s_second,
    halo_sems, sems, s_sems,
):
    cols, rows = large_ref.shape[:2]
    row, col = lax.axis_index("rows"), lax.axis_index("cols")
    taps = KSIZE * KSIZE
    buf[...] = jnp.zeros_like(buf)
    buf[:, HALF : HALF + tile_rows, 8 : 8 + tile_cols, :] = d_ref[...]
    flat[...] = jnp.zeros_like(flat)
    greet(row, col, rows, cols)
    big = Reduction(large_ref, large_out, paired, held, first, middle, second, sems)
    little = Reduction(small, small_out, s_paired, s_held, s_first, s_middle, s_second, s_sems)
    wait = halo_cols(buf, halo_sems, row, col, cols, tile_rows, tile_cols)
    big.send_pair()
    kernel_grad(x_ref, d_ref=buf, acc_ref=acc, tile_rows=tile_rows, tile_cols=tile_cols, h=0)
    big.sum_pair()
    wait()
    wait = halo_rows(buf, halo_sems, row, col, rows, tile_rows)
    kernel_grad(x_ref, d_ref=buf, acc_ref=acc, tile_rows=tile_rows, tile_cols=tile_cols, h=1)
    wait()
    patch_size = patches_ref.shape[0]
    part = flat.shape[0] // 2
    for h in range(2):
        conv_windows(buf, w_ref, out, tile_rows, tile_cols, True, h)
        d = out[h].reshape(tile_rows * tile_cols, LANES).astype(bf16)
        base = h * part
        flat[base : base + patch_size, :] = jnp.dot(
            patches_ref[...], d, preferred_element_type=f32
        )
        flat[base + patch_size : base + patch_size + taps, :] = jnp.sum(acc[h], axis=1)
        flat[base + part - 2 : base + part - 1, :] = jnp.sum(d.astype(f32), axis=0, keepdims=True)
        flat[base + part - 1 : base + part, :] = gain_ref[:, h * LANES : (h + 1) * LANES]
        if h == 0:
            big.sum_cols()
    for n in range(cols * rows):
        block = small.shape[2]
        small[n // rows, n % rows] = flat[n * block : (n + 1) * block, :]
    little.send_pair()
    big.sum_rows()
    little.sum_pair()
    big.spread_cols()
    little.sum_cols()
    little.sum_rows()
    little.spread_cols()
    little.spread_pair()
    big.spread_pair()


def closing(large, x, d_mixed, taps_w, patches_t, grad_gain, rows, cols):
    _, tile_rows, tile_cols, _ = d_mixed.shape
    n = large.size // (rows * cols * LANES)
    large = large.reshape(cols, rows, n, LANES)
    pieces = rows * cols
    needed = 2 * (patches_t.shape[0] + KSIZE * KSIZE + 2)
    m = pl.cdiv(needed, pieces * 8) * 8
    vmem = pl.BlockSpec(memory_space=pltpu.VMEM)
    return pl.pallas_call(
        functools.partial(closing_kernel, tile_rows, tile_cols),
        out_shape=[struct(cols, rows, n, LANES, dtype=bf16), struct(cols, rows, m, LANES)],
        in_specs=[vmem] * 6,
        out_specs=[vmem] * 2,
        scratch_shapes=[
            pltpu.VMEM((2, tile_rows + 2 * HALF, tile_cols + 16, LANES), f32),
            pltpu.VMEM((2, KSIZE * KSIZE, 8, LANES), f32),
            pltpu.VMEM((2, tile_rows, tile_cols, LANES), f32),
            pltpu.VMEM((pieces * m, LANES), f32),
            pltpu.VMEM((cols, rows, m, LANES), f32),
            pltpu.VMEM((cols // 2, rows, n, LANES), bf16),
            pltpu.VMEM((cols // 2, rows, n, LANES), bf16),
            pltpu.VMEM((cols // 2, rows, n, LANES), bf16),
            pltpu.VMEM((rows, n, LANES), bf16),
            pltpu.VMEM((rows, n, LANES), bf16),
            pltpu.VMEM((cols // 2, rows, m, LANES), f32),
            pltpu.VMEM((cols // 2, rows, m, LANES), f32),
            pltpu.VMEM((cols // 2, rows, m, LANES), f32),
            pltpu.VMEM((rows, m, LANES), f32),
            pltpu.VMEM((rows, m, LANES), f32),
            pltpu.SemaphoreType.DMA((2, 4)),
            pltpu.SemaphoreType.DMA((2, 6, max(rows, cols))),
            pltpu.SemaphoreType.DMA((2, 6, max(rows, cols))),
        ],
        compiler_params=pltpu.CompilerParams(
            collective_id=2, has_side_effects=True, vmem_limit_bytes=VMEM_LIMIT
        ),
        name="closing",
    )(large, x, d_mixed, taps_w, patches_t, grad_gain)


def combine(stats):
    peak = jnp.max(stats[:, 0], axis=0)
    factor = jnp.exp2(stats[:, 0] - peak[None])
    return jnp.stack(
        [peak, jnp.sum(stats[:, 1] * factor, axis=0), jnp.sum(stats[:, 2] * factor, axis=0)]
    )


def stats_kernel(rows, cols, x_ref, out_ref, first, second, sems):
    row, col = lax.axis_index("rows"), lax.axis_index("cols")
    greet(row, col, rows, cols)
    copies = []
    first[0] = x_ref[...]
    for p in range(1, cols):
        there = (row, lax.rem(col + p, cols))
        copies.append(push(x_ref, first.at[p], sems, 0, p, there))
    for p in range(1, cols):
        await_into(first.at[p], sems, 0, p, (row, lax.rem(col + cols - p, cols)))
    second[0] = combine(first[...])
    for p in range(1, rows):
        there = (lax.rem(row + p, rows), col)
        copies.append(push(second.at[0], second.at[p], sems, 1, p, there))
    for p in range(1, rows):
        await_into(second.at[p], sems, 1, p, (lax.rem(row + rows - p, rows), col))
    total = combine(second[...])
    out_ref[0] = total[0] + jnp.log2(total[1])
    out_ref[1] = total[2] / total[1]
    for copy in copies:
        copy.wait_send()


def mesh_stats(x, rows, cols):
    vmem = pl.BlockSpec(memory_space=pltpu.VMEM)
    return pl.pallas_call(
        functools.partial(stats_kernel, rows, cols),
        out_shape=struct(2, *x.shape[1:]),
        in_specs=[vmem],
        out_specs=vmem,
        scratch_shapes=[
            pltpu.VMEM((cols,) + x.shape, f32),
            pltpu.VMEM((rows,) + x.shape, f32),
            pltpu.SemaphoreType.DMA((2, 2, max(rows, cols))),
        ],
        compiler_params=pltpu.CompilerParams(
            collective_id=1, has_side_effects=True, vmem_limit_bytes=VMEM_LIMIT
        ),
        name="stats",
    )(x)


def format_kernel(large_ref, attended_ref, grad_q_ref, grad_kv_ref):
    attended_ref[...] = large_ref[0, 0].astype(f32)
    grad_q_ref[...] = large_ref[0, 1].astype(f32)
    head = pl.program_id(0)
    width = grad_kv_ref.shape[1] // 2
    keys = pl.ds(pl.multiple_of(head * LANES, LANES), LANES)
    values = pl.ds(pl.multiple_of(width + head * LANES, LANES), LANES)
    grad_kv_ref[:, keys] = large_ref[0, 2].astype(f32)
    grad_kv_ref[:, values] = large_ref[0, 3].astype(f32)


def head_spec(shape):
    return pl.BlockSpec((1,) + shape, lambda n: (n, 0, 0))


def whole_spec(shape):
    return pl.BlockSpec(shape, lambda n: (0,) * len(shape))


def struct(*shape, dtype=f32):
    return jax.ShapeDtypeStruct(shape, dtype)


def per_device(
    pixels, patch_weight, patch_bias, conv_kernel, norm_gain, kv_weight, latents, d_attended
):
    tile_rows = pixels.shape[1] // PATCH
    tile_cols = pixels.shape[2] // PATCH
    tokens = tile_rows * tile_cols
    channels = patch_weight.shape[1]
    count, model_dim = latents.shape
    parts = count // LANES
    rows, cols = lax.axis_size("rows"), lax.axis_size("cols")
    patches_t = patch_columns(pixels)
    pad_rows, pad_cols = tile_rows + 2 * HALF, tile_cols + 16
    vmem = pl.BlockSpec(memory_space=pltpu.VMEM)
    x = pl.pallas_call(
        functools.partial(embed_kernel, rows, cols, tile_rows, tile_cols),
        out_shape=struct(2, pad_rows, pad_cols, LANES),
        in_specs=[vmem] * 3,
        out_specs=vmem,
        scratch_shapes=[
            pltpu.VMEM((2, pad_rows, pad_cols, LANES), f32),
            pltpu.SemaphoreType.DMA((2, 4)),
        ],
        compiler_params=pltpu.CompilerParams(
            collective_id=3, has_side_effects=True, vmem_limit_bytes=VMEM_LIMIT
        ),
        name="embed",
    )(patches_t, patch_weight, patch_bias.reshape(1, channels))

    taps = KSIZE * KSIZE
    taps_w = conv_kernel.reshape(taps, 2, LANES).transpose(1, 0, 2)
    taps_w = jnp.broadcast_to(taps_w[:, :, None, :], (2, taps, 8, LANES))
    gain = norm_gain.reshape(1, channels)
    kv = kv_weight.reshape(channels, 2, HEADS, LANES).transpose(2, 0, 1, 3)
    kv = kv.reshape(HEADS, channels, 2 * LANES)
    kvt = kv.transpose(0, 2, 1)
    q = latents.reshape(count, HEADS, LANES).transpose(1, 0, 2)
    qt = q.transpose(0, 2, 1)
    da = d_attended.reshape(count, HEADS, LANES).transpose(1, 0, 2)
    dat = da.transpose(0, 2, 1)
    params = pltpu.CompilerParams(vmem_limit_bytes=VMEM_LIMIT)
    mixed, proj, stats, weighted = pl.pallas_call(
        functools.partial(forward_kernel, tile_rows, tile_cols),
        grid=(HEADS,),
        in_specs=[
            whole_spec((2, pad_rows, pad_cols, LANES)),
            whole_spec((2, taps, 8, LANES)),
            whole_spec((1, channels)),
            head_spec((channels, 2 * LANES)),
            head_spec((LANES, count)),
            head_spec((LANES, count)),
        ],
        out_specs=[
            whole_spec((2, tile_rows, tile_cols, LANES)),
            head_spec((tokens, 2 * LANES)),
            pl.BlockSpec((3, 1, 1, count), lambda n: (0, n, 0, 0)),
            head_spec((LANES, count)),
        ],
        out_shape=[
            struct(2, tile_rows, tile_cols, LANES),
            struct(HEADS, tokens, 2 * LANES, dtype=bf16),
            struct(3, HEADS, 1, count),
            struct(HEADS, LANES, count),
        ],
        scratch_shapes=[pltpu.VMEM((tokens, channels), bf16), pltpu.VMEM((tokens, count), f32)],
        compiler_params=params,
        name="forward",
    )(x, taps_w, gain, kv, qt, dat)
    shared = mesh_stats(stats, rows, cols)
    large, d_mixed, grad_gain = pl.pallas_call(
        functools.partial(backward_kernel, tile_rows, tile_cols),
        grid=(HEADS,),
        in_specs=[
            whole_spec((2, tile_rows, tile_cols, LANES)),
            whole_spec((1, channels)),
            head_spec((tokens, 2 * LANES)),
            head_spec((LANES, count)),
            head_spec((count, LANES)),
            head_spec((LANES, count)),
            head_spec((count, LANES)),
            head_spec((2 * LANES, channels)),
            pl.BlockSpec((2, 1, 1, count), lambda n: (0, n, 0, 0)),
            pl.BlockSpec((3, 1, 1, count), lambda n: (0, n, 0, 0)),
            head_spec((LANES, count)),
        ],
        out_specs=[
            pl.BlockSpec((1, 4, channels, LANES), lambda n: (n, 0, 0, 0)),
            whole_spec((2, tile_rows, tile_cols, LANES)),
            whole_spec((1, channels)),
        ],
        out_shape=[
            struct(HEADS, 4, channels, LANES, dtype=bf16),
            struct(2, tile_rows, tile_cols, LANES),
            struct(1, channels),
        ],
        scratch_shapes=[
            pltpu.VMEM((tokens, channels), bf16),
            pltpu.VMEM((8, LANES), bf16),
            pltpu.VMEM((tokens, channels), f32),
        ],
        compiler_params=params,
        name="backward",
    )(mixed, gain, proj, qt, q, dat, da, kvt, shared, stats, weighted)
    large, small = closing(large, x, d_mixed, taps_w, patches_t, grad_gain, rows, cols)
    attended, grad_latents, grad_kv = pl.pallas_call(
        format_kernel,
        grid=(HEADS,),
        in_specs=[pl.BlockSpec((1, 4, count, LANES), lambda n: (n, 0, 0, 0))],
        out_specs=[
            pl.BlockSpec((count, LANES), lambda n: (0, n)),
            pl.BlockSpec((count, LANES), lambda n: (0, n)),
            whole_spec((channels, 2 * model_dim)),
        ],
        out_shape=[
            struct(count, model_dim), struct(count, model_dim), struct(channels, 2 * model_dim)
        ],
        name="outputs",
    )(large.reshape(HEADS, 4, count, LANES))
    half_rows = small.size // (2 * LANES)
    small = small.reshape(2, half_rows, LANES).transpose(1, 0, 2).reshape(half_rows, channels)
    size = patches_t.shape[0]
    return (
        attended,
        grad_latents,
        grad_kv,
        small[-1],
        small[size : size + taps],
        small[:size],
        small[-2],
    )


def solution(mesh):
    return jax.shard_map(
        per_device,
        mesh=mesh,
        in_specs=(P(None, "rows", "cols"), P(), P(), P(), P(), P(), P(), P()),
        out_specs=(P(), P(), P(), P(), P(), P(), P()),
        check_vma=False,
    )
```
